128 devices in a mesh: seg: 8 (over y, z_lo), space: 16 (over x, z_hi, core).
Axes of the slice: x: 4, y: 4, z: 4 (z_hi: 2, z_lo: 2; z = z_hi * 2 + z_lo), core: 2. Of those that a mesh axis runs over, the one named last changes fastest.
Arguments:
- vorticity: float32 [8, 2048, 2048], P('seg', 'space'), may hold values from -6 to 6
Outputs:
- gradient: float32 [8, 2048, 2048], P('seg', 'space')
- residual_spectrum: float32 [8, 2, 2048, 2048], P('seg', None, None, 'space')
The draws below stay inside these ranges and needn't reach their ends.
All inputs are finite; a program needn't handle non-finite values.
Results may differ from the reference program's by a relative error of at most 0.0001.
Values sent between devices are 32-bit elements; how exact they have to be, the bound alone decides.
A program may use at most 128 MiB of HBM per device.

```python
import math
import jax
import jax.numpy as jnp
from jax import lax

N = 2048
STEPS = 1
SEGS = 8
ROWS = 128


def shard_levels(key, shape, split, least, largest):
    def one(axis_at, parts):
        heights = jax.random.uniform(jax.random.fold_in(jax.random.fold_in(key, 6), axis_at), (parts,), jnp.float32, least / len(split), largest / len(split))
        return jnp.repeat(jnp.exp(heights), shape[axis_at] // parts).reshape((-1,) + (1,) * (len(shape) - axis_at - 1))

    level = one(*split[0])
    for cut in split[1:]:
        level = level * one(*cut)
    return level


def normal_values(stream_key, extent, deviation, reach, shards=(), kind=jnp.bfloat16):
    values = jax.random.normal(stream_key, extent, jnp.float32) * deviation
    if len(shards) > 0:
        values = shard_levels(stream_key, extent, shards, -0.22, 0.18) * values
    return jnp.clip(values, min=-reach, max=reach).astype(kind)


def setup_inputs(seed: int = 0) -> dict:
    key_of = jax.random.split(jax.random.key(seed), 2)
    return {
        "vorticity": normal_values(key_of[0], (SEGS, N, N), 1.0, 6.0, ((0, 8), (1, 16)), jnp.float32),
    }


time_step = 0.3
drag_rate = 0.05
force_amp = 0.8
forcing_wave = 4

def wave_tables():
    wave_index = jnp.arange(N, dtype=jnp.int32)
    wave_num = jnp.where(wave_index < N // 2, wave_index, wave_index - N)
    deriv_num = jnp.where(wave_index == N // 2, 0, wave_num).astype(jnp.float32)
    wave_float = wave_num.astype(jnp.float32)
    wave_sq = wave_float[:, None] * wave_float[:, None] + wave_float[None, :] * wave_float[None, :]
    inv_sq = jnp.where(wave_sq > 0, 1.0 / jnp.maximum(wave_sq, 1.0), 0.0)
    decay_fac = jnp.exp(-time_step * (drag_rate + 9.0 * wave_sq / (N * N)))
    keep_line = 3 * jnp.abs(wave_num) <= N
    keep_mask = (keep_line[:, None] & keep_line[None, :]).astype(jnp.float32)
    nl_factor = time_step * decay_fac * keep_mask
    columns = jnp.arange(N, dtype=jnp.float32)
    forcing = force_amp * jnp.cos(forcing_wave * 2.0 * math.pi * columns / N)
    force_field = jnp.broadcast_to(forcing[None, :], (N, N))
    force_hat = time_step * decay_fac * jnp.fft.fft2(force_field)
    return (deriv_num[:, None], deriv_num[None, :], inv_sq, decay_fac, nl_factor, force_hat)

def column_order():
    column = jnp.arange(N, dtype=jnp.int32)
    block = column // ROWS
    slot = column % ROWS
    half_rows = ROWS // 2
    upper = jnp.where(column == half_rows, N // 2, N - block * half_rows - (slot - half_rows))
    return jnp.where(slot < half_rows, block * half_rows + slot, upper).astype(jnp.int32)

def inverse_real(spectrum):
    return jnp.real(jnp.fft.ifft2(spectrum))

def advance(spectrum, tables):
    kx_deriv, ky_deriv, inv_sq, decay_fac, nl_factor, force_hat = tables
    stream = spectrum * inv_sq
    vel_x = inverse_real(1j * ky_deriv * stream)
    vel_y = inverse_real(-1j * kx_deriv * stream)
    grad_x = inverse_real(1j * kx_deriv * spectrum)
    grad_y = inverse_real(1j * ky_deriv * spectrum)
    nonlinear = vel_x * grad_x + vel_y * grad_y
    return decay_fac * spectrum - nl_factor * jnp.fft.fft2(nonlinear) + force_hat

def flow_end(vort_field, tables):
    spectrum = jnp.fft.fft2(vort_field)
    for moment in range(STEPS):
        spectrum = advance(spectrum, tables)
    return spectrum

def reference(vorticity):
    tables = wave_tables()
    start_spec = lax.map(jnp.fft.fft2, vorticity)
    end_spec = lax.map(lambda vort_field: flow_end(vort_field, tables), vorticity)
    res_spec = jnp.roll(end_spec, 1, axis=0) - start_spec
    residual = lax.map(inverse_real, res_spec)
    next_res = jnp.roll(residual, -1, axis=0)

    def segment_grad(pair_args):
        vort_field, seed_field = pair_args
        ignored, pullback = jax.vjp(lambda value_in: inverse_real(flow_end(value_in, tables)), vort_field)
        return pullback(seed_field)[0]
    adjoint = lax.map(segment_grad, (vorticity, next_res))
    gradient = (adjoint - residual).astype(jnp.float32)
    stacked = jnp.stack([jnp.real(res_spec), jnp.imag(res_spec)], axis=1) / N
    spectrum_out = jnp.take(stacked, column_order(), axis=3).astype(jnp.float32)
    return (gradient, spectrum_out)
```

```python
import functools
import math

import jax
import jax.numpy as jnp
import ml_dtypes
import numpy as np
from jax import lax
from jax.experimental import pallas as pl
from jax.experimental.pallas import tpu as pltpu
from jax.sharding import PartitionSpec as P

N = 2048
SLABS = 16
LANES = 128
ROWS_KY = 72
PAIR = 2 * ROWS_KY
TIME_STEP = 0.3
DRAG = 0.05
FORCE_AMP = 0.8
FORCING_WAVE = 4
MESH = pl.DeviceIdType.MESH
F32 = jnp.float32
BF16 = jnp.bfloat16


def split_table(table):
    high = table.astype(np.float32).astype(ml_dtypes.bfloat16)
    low = (table - high.astype(np.float64)).astype(np.float32).astype(ml_dtypes.bfloat16)
    return high, low


def slot_wave(j, d, r):
    if r < 4:
        return j + 16 * (4 * d + r)
    return (16 - j if j else 8) + 16 * (4 * d + r - 4)


@functools.cache
def row_tables():
    a = np.arange(LANES)
    forward = np.zeros((8, 16, 2, 8, 2, LANES))
    inverse = np.zeros((8, 2, LANES, 16, 2, 8))
    wave = np.zeros((8, 16, 8))
    for j in range(8):
        for d in range(16):
            for r in range(8):
                k = slot_wave(j, d, r)
                wave[j, d, r] = k
                c = np.cos(2 * np.pi * ((a * k) % N) / N)
                s = np.sin(2 * np.pi * ((a * k) % N) / N)
                if j == 0:
                    part = 0 if r < 4 else 1
                    forward[j, d, 0, r, part] = c
                    forward[j, d, 1, r, part] = -s
                    inverse[j, part, :, d, 0, r] = 2 * c
                    inverse[j, part, :, d, 1, r] = -2 * s
                    if k == 0:
                        alternate = 1.0 - 2.0 * (a % 2)
                        forward[j, d, 1, r, part] = alternate
                        inverse[j, part, :, d, 0, r] = 1.0
                        inverse[j, part, :, d, 1, r] = alternate
                else:
                    sign = 1.0 if r < 4 else -1.0
                    forward[j, d, 0, r, 0] = c
                    forward[j, d, 0, r, 1] = sign * s
                    forward[j, d, 1, r, 0] = -s
                    forward[j, d, 1, r, 1] = sign * c
                    inverse[j, 0, :, d, 0, r] = c
                    inverse[j, 0, :, d, 1, r] = -s
                    inverse[j, 1, :, d, 0, r] = sign * s
                    inverse[j, 1, :, d, 1, r] = sign * c
    inverse /= N
    dwave = wave[:, :, None, :, None, None]
    forward_dy = np.stack([-forward[:, :, 1], forward[:, :, 0]], axis=2) * dwave
    inverse_dy = np.stack([inverse[..., 1, :], -inverse[..., 0, :]], axis=-2) * wave[:, None, None, :, None, :]
    shape = (8, 256, 256)
    outs = []
    for table in (forward, forward_dy, inverse, inverse_dy):
        high, low = split_table(table.reshape(shape))
        outs.append(np.stack([high, low]))
    return np.stack(outs)


@functools.cache
def col_tables():
    a = np.arange(LANES)
    angle = 2 * np.pi * (np.outer(a, a) % LANES) / LANES
    c, s = np.cos(angle), np.sin(angle)
    forward = np.block([[c, -s], [s, c]])
    inverse = np.block([[c, s], [-s, c]]) / N
    mats = np.stack([np.stack(split_table(m)) for m in (forward, inverse)])
    angle = 2 * np.pi * np.outer(np.arange(16), a) / N
    twiddle = np.stack([np.cos(angle), np.sin(angle)], axis=1)
    twiddle = np.broadcast_to(twiddle[:, :, None, :], (16, 2, 8, LANES)).astype(np.float32)
    return mats, np.ascontiguousarray(twiddle)


@functools.cache
def flip_tables():
    eye = np.eye(LANES)
    first = np.concatenate([eye, eye[(LANES - np.arange(LANES)) % LANES]], axis=1)
    other = np.concatenate([eye, eye[LANES - 1 - np.arange(LANES)]], axis=1)
    return (np.stack([first, other]) / N).astype(ml_dtypes.bfloat16)


@functools.cache
def slot_table():
    return np.array([[slot_wave(j, 0, r) for r in range(8)] for j in range(8)], np.int32)


def times_root(re, im, k, n, sign):
    k = k % n
    if im is None:
        if k == 0:
            return re, None
        angle = sign * 2 * math.pi * k / n
        if 4 * k == n:
            return None, (re if sign > 0 else -re)
        return re * math.cos(angle), re * math.sin(angle)
    if k == 0:
        return re, im
    if 2 * k == n:
        return -re, -im
    if 4 * k == n:
        return (-im, re) if sign > 0 else (im, -re)
    if 4 * k == 3 * n:
        return (im, -re) if sign > 0 else (-im, re)
    angle = sign * 2 * math.pi * k / n
    c, s = math.cos(angle), math.sin(angle)
    if 8 * k == n or 8 * k == 3 * n or 8 * k == 5 * n or 8 * k == 7 * n:
        m = abs(c)
        rm, imm = re * m, im * m
        sc, ss = (1 if c > 0 else -1), (1 if s > 0 else -1)
        first = (rm if sc > 0 else -rm) - imm if ss > 0 else (rm if sc > 0 else -rm) + imm
        second = (imm if sc > 0 else -imm) + rm if ss > 0 else (imm if sc > 0 else -imm) - rm
        return first, second
    return re * c - im * s, re * s + im * c


def complex_fft(values, sign):
    n = len(values)
    if n == 1:
        return values
    even = complex_fft(values[0::2], sign)
    odd = complex_fft(values[1::2], sign)
    outs = [None] * n
    for k in range(n // 2):
        re, im = times_root(odd[k][0], odd[k][1], k, n, sign)
        outs[k] = (even[k][0] + re, even[k][1] + im)
        outs[k + n // 2] = (even[k][0] - re, even[k][1] - im)
    return outs


def real_fft(values):
    n = len(values)
    if n == 2:
        return [(values[0] + values[1], None), (values[0] - values[1], None)]
    even, odd = real_fft(values[0::2]), real_fft(values[1::2])
    half = n // 2
    outs = [None] * (half + 1)
    outs[0] = (even[0][0] + odd[0][0], None)
    outs[half] = (even[0][0] - odd[0][0], None)
    for k in range(1, half // 2 + 1):
        if 4 * k == n:
            outs[k] = (even[k][0], -odd[k][0])
            continue
        re, im = times_root(odd[k][0], odd[k][1], k, n, -1)
        outs[k] = (even[k][0] + re, even[k][1] + im)
        outs[half - k] = (even[k][0] - re, im - even[k][1])
    return outs


def real_inverse(values):
    half = len(values) - 1
    n = 2 * half
    if n == 2:
        return [values[0][0] + values[1][0], values[0][0] - values[1][0]]
    even, odd = [None] * (half // 2 + 1), [None] * (half // 2 + 1)
    even[0] = (values[0][0] + values[half][0], None)
    odd[0] = (values[0][0] - values[half][0], None)
    for k in range(1, half // 2 + 1):
        if 4 * k == n:
            even[k] = (values[k][0] * 2.0, None)
            odd[k] = (values[k][1] * -2.0, None)
            continue
        (ar, ai), (br, bi) = values[k], values[half - k]
        even[k] = (ar + br, ai - bi)
        odd[k] = times_root(ar - br, ai + bi, k, n, 1)
    low, high = real_inverse(even), real_inverse(odd)
    outs = [None] * n
    outs[0::2] = low
    outs[1::2] = high
    return outs


def split(values):
    high = values.astype(BF16)
    return high, (values - high.astype(F32)).astype(BF16)


def dot(a, b):
    return jnp.dot(a, b, preferred_element_type=F32)


def table_times(high, low, values):
    vh, vl = split(values)
    return dot(high, vh) + (dot(low, vh) + dot(high, vl))


def times_table(values, high, low):
    vh, vl = split(values)
    return dot(vh, high) + (dot(vh, low) + dot(vl, high))


def loop(count, step):
    lax.fori_loop(0, count, lambda i, c: (step(i), c)[1], 0)


def tile(t):
    return pl.ds(pl.multiple_of(t * 8, 8), 8)


def row_forward(load, mat, scratch, out):
    def first(t):
        spectrum = real_fft(load(t))
        scratch[0, tile(t), :] = spectrum[0][0]
        scratch[0, pl.ds(pl.multiple_of(LANES + t * 8, 8), 8), :] = spectrum[8][0]
        for j in range(1, 8):
            scratch[j, tile(t), :] = spectrum[j][0]
            scratch[j, pl.ds(pl.multiple_of(LANES + t * 8, 8), 8), :] = spectrum[j][1]

    def second(j):
        result = table_times(mat[0, j], mat[1, j], scratch[j])
        out[:, j] = result.reshape(16, 2, 8, LANES)

    loop(16, first)
    loop(8, second)


def row_inverse(load, mat, scratch, emit):
    def first(j):
        scratch[j] = table_times(mat[0, j], mat[1, j], load(j))

    def second(t):
        upper = pl.ds(pl.multiple_of(LANES + t * 8, 8), 8)
        spectrum = [(scratch[0, tile(t), :], None)]
        spectrum += [(scratch[j, tile(t), :], scratch[j, upper, :]) for j in range(1, 8)]
        spectrum.append((scratch[0, upper, :], None))
        emit(t, real_inverse(spectrum))

    loop(8, first)
    loop(16, second)


def col_forward(received, first_mask, mats, twiddle, scratch, emit):
    def transform(values, at):
        spectrum = complex_fft(values, -1)
        for k in range(16):
            re, im = spectrum[k]
            if k:
                c, s = twiddle[k, 0], twiddle[k, 1]
                re, im = re * c + im * s, im * c - re * s
            rows = pl.ds(pl.multiple_of((k % 2) * ROWS_KY + at * 8, 8), 8)
            scratch[k // 2, rows, 0:LANES] = re
            scratch[k // 2, rows, LANES : 2 * LANES] = im

    zero = jnp.zeros((8, LANES), F32)
    transform(
        [(received[b, 0, 0], jnp.where(first_mask, 0.0, received[b, 0, 1])) for b in range(16)], 0
    )
    transform([(jnp.where(first_mask, received[b, 0, 1], 0.0), zero) for b in range(16)], 8)
    loop(7, lambda i: transform([(received[b, i + 1, 0], received[b, i + 1, 1]) for b in range(16)], i + 1))
    loop(8, lambda c: emit(c, times_table(scratch[c], mats[0, 0], mats[0, 1])))


def col_inverse(load, first_mask, mats, twiddle, scratch, out):
    def first(c):
        scratch[c] = times_table(load(c), mats[1, 0], mats[1, 1])

    def transform(at):
        values = []
        for k in range(16):
            rows = pl.ds(pl.multiple_of((k % 2) * ROWS_KY + at * 8, 8), 8)
            re = scratch[k // 2, rows, 0:LANES]
            im = scratch[k // 2, rows, LANES : 2 * LANES]
            if k:
                c, s = twiddle[k, 0], twiddle[k, 1]
                re, im = re * c - im * s, im * c + re * s
            values.append((re, im))
        return complex_fft(values, 1)

    def second(j):
        for b, (re, im) in enumerate(transform(j)):
            out[b, j, 0] = re
            out[b, j, 1] = im

    loop(8, first)
    extra = transform(8)
    for b in range(16):
        out[b, 0, 0] = extra[b][0]
    for b, (re, im) in enumerate(transform(0)):
        out[b, 0, 1] = jnp.where(first_mask, out[b, 0, 0], im)
        out[b, 0, 0] = re
    loop(7, lambda i: second(i + 1))


def bit(value, k):
    return (value // (1 << k)) % 2


def partner(me, i):
    core = me % 2
    offset = i * (1 - core) + (16 - i) * core
    return sum(((bit(me, k) + bit(offset, k)) % 2) * (1 << k) for k in range(4))


def kernel(
    vort, row_hbm, col_mats, twiddle, flips, ky_ref,
    grad, resid,
    rowm, grid_a, grid_u, grid_v, grid_wx, grid_wy, sends, recvs, local_b,
    row_s, col_s, w_spec, e_spec, adj, next_start, prev_end,
    dx_t, linv_t, decay_t, nlf_t, flat,
    table_sem, own_sem, send_sem, recv_sem, seg_send, seg_recv,
):
    me = lax.axis_index("space")
    seg = lax.axis_index("seg")
    after, before = (seg + 1) % 8, (seg + 7) % 8
    rows_in_tile = lax.broadcasted_iota(jnp.int32, (8, LANES), 0)
    first_mask = (rows_in_tile == 0) & (jnp.zeros((8, LANES), jnp.int32) + me == 0)

    def table_copy(i):
        return pltpu.make_async_copy(row_hbm.at[i], rowm.at[i], table_sem.at[i])

    for i in (0, 3, 2, 1):
        table_copy(i).start()

    barrier = pltpu.get_barrier_semaphore()
    loop(15, lambda i: pl.semaphore_signal(
        barrier, inc=1, device_id={"space": partner(me, i + 1)}, device_id_type=MESH))
    for s in (after, before):
        pl.semaphore_signal(barrier, inc=1, device_id={"seg": s}, device_id_type=MESH)

    def copy_to(f, i):
        p = partner(me, i)
        return pltpu.make_async_remote_copy(
            src_ref=sends.at[f, p], dst_ref=recvs.at[f, me],
            send_sem=send_sem.at[f, i - 1], recv_sem=recv_sem.at[f, i - 1],
            device_id={"space": p}, device_id_type=MESH)

    def own_copy(f):
        return pltpu.make_async_copy(sends.at[f, me], recvs.at[f, me], own_sem.at[f])

    def start(f):
        own_copy(f).start()
        loop(15, lambda i: copy_to(f, i + 1).start())

    def finish(f):
        own_copy(f).wait()

        def one(i):
            copy = copy_to(f, i + 1)
            copy.wait_recv()
            copy.wait_send()

        loop(15, one)

    def seg_copy(i):
        source, target, s = ((w_spec, next_start, before), (e_spec, prev_end, after))[i]
        return pltpu.make_async_remote_copy(
            src_ref=source, dst_ref=target, send_sem=seg_send.at[i], recv_sem=seg_recv.at[i],
            device_id={"seg": s}, device_id_type=MESH)

    for b in range(16):
        grid_a[b] = vort[:, b * LANES : (b + 1) * LANES].T
    table_copy(0).wait()
    row_forward(lambda t: [grid_a[b, tile(t), :] for b in range(16)], rowm.at[0], row_s, sends.at[0])
    pl.semaphore_wait(barrier, 17)
    start(0)

    def stacked(f):
        return lambda j: sends[f, :, j].reshape(256, LANES)

    def arrived(f):
        return lambda j: recvs[f, :, j].reshape(256, LANES)

    def keep(ref):
        def emit(t, tiles):
            for b in range(16):
                ref[b, tile(t), :] = tiles[b]
        return emit

    table_copy(3).wait()
    row_inverse(stacked(0), rowm.at[3], row_s, keep(grid_wy))

    flat[...] = jnp.zeros_like(flat)

    def make_tables(c):
        rows = lax.broadcasted_iota(jnp.int32, (PAIR, LANES), 0)
        lanes = lax.broadcasted_iota(jnp.int32, (PAIR, LANES), 1)
        k = 2 * c + jnp.where(rows >= ROWS_KY, 1, 0) + 16 * lanes
        kx = jnp.where(k < N // 2, k, k - N)
        ky = ky_ref[...]
        kxf = kx.astype(F32)
        square = kxf * kxf + ky * ky
        decay = jnp.exp(-TIME_STEP * (DRAG + 9.0 * square / (N * N)))
        dx_t[c] = jnp.where(kx == -(N // 2), 0.0, kxf)
        linv_t[c] = jnp.where(square > 0.0, 1.0 / jnp.maximum(square, 1.0), 0.0)
        decay_t[c] = decay
        inside = (3.0 * jnp.abs(kxf) <= N) & (3.0 * jnp.abs(ky) <= N)
        nlf_t[c] = jnp.where(inside, TIME_STEP * decay, 0.0)

    loop(8, make_tables)

    finish(0)

    def put_w(c, value):
        w_spec[c] = value

    col_forward(recvs.at[0], first_mask, col_mats, twiddle, col_s, put_w)
    seg_copy(0).start()

    def two(re, im):
        return jnp.concatenate([re, im], axis=1)

    def halves(ref, c):
        return ref[c, :, 0:LANES], ref[c, :, LANES : 2 * LANES]

    def psi_hat(c):
        re, im = halves(w_spec, c)
        linv = linv_t[c]
        return two(linv * re, linv * im)

    def v_hat(c):
        re, im = halves(w_spec, c)
        factor = linv_t[c] * dx_t[c]
        return two(factor * im, -factor * re)

    def wx_hat(c):
        re, im = halves(w_spec, c)
        factor = dx_t[c]
        return two(-factor * im, factor * re)

    for f, hat in ((1, psi_hat), (2, v_hat), (3, wx_hat)):
        col_inverse(hat, first_mask, col_mats, twiddle, col_s, sends.at[f])
        start(f)

    finish(1)
    row_inverse(arrived(1), rowm.at[3], row_s, keep(grid_u))
    table_copy(2).wait()
    finish(2)
    row_inverse(arrived(2), rowm.at[2], row_s, keep(grid_v))
    finish(3)

    def nonlinear(t, tiles):
        for b in range(16):
            grid_wx[b, tile(t), :] = tiles[b]
            grid_a[b, tile(t), :] = (
                grid_u[b, tile(t), :] * tiles[b] + grid_v[b, tile(t), :] * grid_wy[b, tile(t), :]
            )

    row_inverse(arrived(3), rowm.at[2], row_s, nonlinear)
    row_forward(lambda t: [grid_a[b, tile(t), :] for b in range(16)], rowm.at[0], row_s, sends.at[4])
    start(4)
    table_copy(1).wait()
    seg_copy(0).wait_recv()
    finish(4)

    def put_end(c, value):
        re, im = halves(w_spec, c)
        decay, nlf, dx = decay_t[c], nlf_t[c], dx_t[c]
        forced = (dx == 0.0) & (nlf > 0.0) & (ky_ref[...] == float(FORCING_WAVE))
        force = jnp.where(forced, TIME_STEP * FORCE_AMP * (N * N / 2.0) * decay, 0.0)
        end_re = decay * re - nlf * value[:, 0:LANES] + force
        end_im = decay * im - nlf * value[:, LANES : 2 * LANES]
        e_spec[c] = two(end_re, end_im)
        next_re, next_im = halves(next_start, c)
        adj[c] = two(end_re - next_re, end_im - next_im)

    col_forward(recvs.at[4], first_mask, col_mats, twiddle, col_s, put_end)

    def weight_hat(c):
        re, im = halves(adj, c)
        nlf = nlf_t[c]
        return two(nlf * re, nlf * im)

    col_inverse(weight_hat, first_mask, col_mats, twiddle, col_s, sends.at[5])
    start(5)
    seg_copy(1).start()
    finish(5)
    row_inverse(arrived(5), rowm.at[2], row_s, keep(grid_a))

    def product(ref):
        return lambda t: [grid_a[b, tile(t), :] * ref[b, tile(t), :] for b in range(16)]

    row_forward(product(grid_u), rowm.at[0], row_s, sends.at[6])
    start(6)
    row_forward(product(grid_wx), rowm.at[1], row_s, sends.at[7])
    start(7)
    row_forward(product(grid_wy), rowm.at[0], row_s, sends.at[8])
    start(8)
    row_forward(product(grid_v), rowm.at[1], row_s, local_b)

    seg_copy(1).wait_recv()
    seg_copy(1).wait_send()
    seg_copy(0).wait_send()

    def make_residual(c):
        prev_re, prev_im = halves(prev_end, c)
        re, im = halves(w_spec, c)
        res_re, res_im = prev_re - re, prev_im - im
        prev_end[c] = two(res_re, res_im)
        adj_re, adj_im = halves(adj, c)
        decay = decay_t[c]
        adj[c] = two(decay * adj_re - res_re, decay * adj_im - res_im)

    loop(8, make_residual)

    slots = slot_table()

    def write_residual(k, mirror, flip):
        for part in range(2):
            lanes = slice(part * LANES, (part + 1) * LANES)
            for j in range(8):
                rows = pl.ds(pl.multiple_of((k % 2) * ROWS_KY + j * 8, 8), 8)
                direct = prev_end[k // 2, rows, lanes]
                rows = pl.ds(pl.multiple_of((mirror % 2) * ROWS_KY + j * 8, 8), 8)
                mirrored = prev_end[mirror // 2, rows, lanes]
                if part:
                    mirrored = -mirrored
                for h in range(2):
                    to = int(slots[j, 4 * h])
                    flat[part, 0, pl.ds(to, 4, stride=16), :] = direct[4 * h : 4 * h + 4]
                    flat[part, 1, pl.ds(64 + to, 4, stride=16), :] = mirrored[4 * h : 4 * h + 4]
            rows = pl.ds(pl.multiple_of((k % 2) * ROWS_KY + 64, 8), 8)
            extra = prev_end[k // 2, rows, lanes]
            flat[part, 0, 64:72, :] = jnp.where(first_mask, extra, 0.0)
            flat[part, 1, 64:72, :] = jnp.where(first_mask, 0.0, flat[part, 1, 64:72, :])
            high, low = split(jnp.concatenate([flat[part, 0], flat[part, 1]], axis=1))
            contract = (((1,), (1,)), ((), ()))
            result = lax.dot_general(flip, high, contract, preferred_element_type=F32)
            result = result + lax.dot_general(flip, low, contract, preferred_element_type=F32)
            resid[part, :, k, :] = result

    write_residual(0, 0, flips[0])
    loop(15, lambda i: write_residual(i + 1, 15 - i, flips[1]))

    finish(6)

    def add_a(c, value):
        re, im = halves(adj, c)
        dx = dx_t[c]
        adj[c] = two(re - dx * value[:, LANES : 2 * LANES], im + dx * value[:, 0:LANES])

    col_forward(recvs.at[6], first_mask, col_mats, twiddle, col_s, add_a)
    finish(7)

    def add_c(c, value):
        re, im = halves(adj, c)
        linv = linv_t[c]
        adj[c] = two(re + linv * value[:, 0:LANES], im + linv * value[:, LANES : 2 * LANES])

    col_forward(recvs.at[7], first_mask, col_mats, twiddle, col_s, add_c)
    finish(8)

    def add_d(c, value):
        re, im = halves(adj, c)
        factor = linv_t[c] * dx_t[c]
        adj[c] = two(re + factor * value[:, LANES : 2 * LANES], im - factor * value[:, 0:LANES])

    col_forward(recvs.at[8], first_mask, col_mats, twiddle, col_s, add_d)
    col_inverse(lambda c: adj[c], first_mask, col_mats, twiddle, col_s, sends.at[9])
    start(9)
    finish(9)

    def total(j):
        return (recvs[9, :, j] + local_b[:, j]).reshape(256, LANES)

    row_inverse(total, rowm.at[2], row_s, keep(grid_a))
    for b in range(16):
        grad[:, b * LANES : (b + 1) * LANES] = grid_a[b].T


def body(vorticity):
    device = lax.axis_index("space")
    col_mats, twiddle = col_tables()
    waves = slot_table().reshape(64, 1).astype(np.float32)
    ky = jnp.asarray(waves) + 64.0 * device.astype(F32)
    ky = jnp.concatenate([ky, jnp.full((8, 1), N // 2, F32)], axis=0)
    ky = jnp.broadcast_to(jnp.concatenate([ky, ky], axis=0), (PAIR, LANES))
    vmem = pl.BlockSpec(memory_space=pltpu.VMEM)
    slab = (16, 8, 2, 8, LANES)
    grid = pltpu.VMEM((16, LANES, LANES), F32)
    spectrum = pltpu.VMEM((8, PAIR, 2 * LANES), F32)
    factor = pltpu.VMEM((8, PAIR, LANES), F32)
    gradient, residual = pl.pallas_call(
        kernel,
        out_shape=(
            jax.ShapeDtypeStruct((LANES, N), F32),
            jax.ShapeDtypeStruct((2, LANES, 16, LANES), F32),
        ),
        in_specs=[vmem, pl.BlockSpec(memory_space=pl.ANY), vmem, vmem, vmem, vmem],
        out_specs=(vmem, vmem),
        scratch_shapes=[
            pltpu.VMEM((4, 2, 8, 256, 256), BF16),
            grid, grid, grid, grid, grid,
            pltpu.VMEM((10,) + slab, F32),
            pltpu.VMEM((10,) + slab, F32),
            pltpu.VMEM(slab, F32),
            pltpu.VMEM((8, 256, LANES), F32),
            spectrum, spectrum, spectrum, spectrum, spectrum, spectrum,
            factor, factor, factor, factor,
            pltpu.VMEM((2, 2, LANES, LANES), F32),
            pltpu.SemaphoreType.DMA((4,)),
            pltpu.SemaphoreType.DMA((10,)),
            pltpu.SemaphoreType.DMA((10, 15)),
            pltpu.SemaphoreType.DMA((10, 15)),
            pltpu.SemaphoreType.DMA((2,)),
            pltpu.SemaphoreType.DMA((2,)),
        ],
        compiler_params=pltpu.CompilerParams(
            collective_id=0, has_side_effects=True, vmem_limit_bytes=60 * 2**20
        ),
        name="orbit_gradient",
    )(vorticity[0], jnp.asarray(row_tables()), jnp.asarray(col_mats), jnp.asarray(twiddle),
      jnp.asarray(flip_tables()), ky)
    return gradient[None], residual.reshape(1, 2, N, LANES)


def solution(mesh):
    return jax.shard_map(
        body,
        mesh=mesh,
        in_specs=(P("seg", "space", None),),
        out_specs=(P("seg", "space", None), P("seg", None, None, "space")),
        check_vma=False,
    )
```

```python
import functools
import math

import jax
import jax.numpy as jnp
import ml_dtypes
import numpy as np
from jax import lax
from jax.experimental import pallas as pl
from jax.experimental.pallas import tpu as pltpu
from jax.sharding import PartitionSpec as P

N = 2048
SLABS = 16
LANES = 128
GROUPS = ((0, 8, 1, 2, 3), (4, 5, 6, 7))
GROUP_J = (0, 4)
ROWS_OF = (40, 32)
FIRST_ROW = (0, 640)
CHUNK = (160, 128)
ALL_ROWS = 16 * (40 + 32)
KEPT = 11
TIME_STEP = 0.3
DRAG = 0.05
FORCE_AMP = 0.8
FORCING_WAVE = 4
MESH = pl.DeviceIdType.MESH
F32 = jnp.float32
BF16 = jnp.bfloat16


def split_table(table):
    high = table.astype(np.float32).astype(ml_dtypes.bfloat16)
    low = (table - high.astype(np.float64)).astype(np.float32).astype(ml_dtypes.bfloat16)
    return high, low


def slot_wave(j, d, r):
    if r < 4:
        return j + 16 * (4 * d + r)
    return (16 - j if j else 8) + 16 * (4 * d + r - 4)


@functools.cache
def row_tables():
    a = np.arange(LANES)
    forward = np.zeros((8, 16, 2, 8, 2, LANES))
    inverse = np.zeros((8, 2, LANES, 16, 2, 8))
    wave = np.zeros((8, 16, 8))
    for j in range(8):
        for d in range(16):
            for r in range(8):
                k = slot_wave(j, d, r)
                wave[j, d, r] = k
                c = np.cos(2 * np.pi * ((a * k) % N) / N)
                s = np.sin(2 * np.pi * ((a * k) % N) / N)
                if j == 0:
                    part = 0 if r < 4 else 1
                    forward[j, d, 0, r, part] = c
                    forward[j, d, 1, r, part] = -s
                    inverse[j, part, :, d, 0, r] = 2 * c
                    inverse[j, part, :, d, 1, r] = -2 * s
                    if k == 0:
                        alternate = 1.0 - 2.0 * (a % 2)
                        forward[j, d, 1, r, part] = alternate
                        inverse[j, part, :, d, 0, r] = 1.0
                        inverse[j, part, :, d, 1, r] = alternate
                else:
                    sign = 1.0 if r < 4 else -1.0
                    forward[j, d, 0, r, 0] = c
                    forward[j, d, 0, r, 1] = sign * s
                    forward[j, d, 1, r, 0] = -s
                    forward[j, d, 1, r, 1] = sign * c
                    inverse[j, 0, :, d, 0, r] = c
                    inverse[j, 0, :, d, 1, r] = -s
                    inverse[j, 1, :, d, 0, r] = sign * s
                    inverse[j, 1, :, d, 1, r] = sign * c
    inverse /= N
    dwave = wave[:, :, None, :, None, None]
    forward_dy = np.stack([-forward[:, :, 1], forward[:, :, 0]], axis=2) * dwave
    inverse_dy = np.stack([inverse[..., 1, :], -inverse[..., 0, :]], axis=-2) * wave[:, None, None, :, None, :]
    shape = (8, 256, 256)
    outs = []
    for table in (forward, forward_dy, inverse, inverse_dy):
        high, low = split_table(table.reshape(shape))
        outs.append(np.stack([high, low]))
    return np.stack(outs)


@functools.cache
def col_tables():
    a = np.arange(LANES)
    angle = 2 * np.pi * (np.outer(a, a) % LANES) / LANES
    c, s = np.cos(angle), np.sin(angle)
    forward = np.block([[c, -s], [s, c]])
    inverse = np.block([[c, s], [-s, c]]) / N
    mats = np.stack([np.stack(split_table(m)) for m in (forward, inverse)])
    angle = 2 * np.pi * np.outer(np.arange(16), a) / N
    twiddle = np.stack([np.cos(angle), np.sin(angle)], axis=1)
    twiddle = np.broadcast_to(twiddle[:, :, None, :], (16, 2, 8, LANES)).astype(np.float32)
    return mats, np.ascontiguousarray(twiddle)


@functools.cache
def flip_tables():
    eye = np.eye(LANES)
    first = np.concatenate([eye, eye[(LANES - np.arange(LANES)) % LANES]], axis=1)
    other = np.concatenate([eye, eye[LANES - 1 - np.arange(LANES)]], axis=1)
    return (np.stack([first, other]) / N).astype(ml_dtypes.bfloat16)


@functools.cache
def slot_table():
    return np.array([[slot_wave(j, 0, r) for r in range(8)] for j in range(8)], np.int32)


@functools.cache
def wave_table():
    table = np.zeros((2, CHUNK[0] + CHUNK[1], LANES), np.float32)
    row = 0
    for group in GROUPS:
        for _ in range(4):
            for j in group:
                table[0, row : row + 8] = (N // 2) if j == 8 else slot_table()[j][:, None]
                table[1, row : row + 8] = 0 if j == 8 else 64
                row += 8
    return table


def times_root(re, im, k, n, sign):
    k = k % n
    if im is None:
        if k == 0:
            return re, None
        angle = sign * 2 * math.pi * k / n
        if 4 * k == n:
            return None, (re if sign > 0 else -re)
        return re * math.cos(angle), re * math.sin(angle)
    if k == 0:
        return re, im
    if 2 * k == n:
        return -re, -im
    if 4 * k == n:
        return (-im, re) if sign > 0 else (im, -re)
    if 4 * k == 3 * n:
        return (im, -re) if sign > 0 else (-im, re)
    angle = sign * 2 * math.pi * k / n
    c, s = math.cos(angle), math.sin(angle)
    if 8 * k == n or 8 * k == 3 * n or 8 * k == 5 * n or 8 * k == 7 * n:
        m = abs(c)
        rm, imm = re * m, im * m
        sc, ss = (1 if c > 0 else -1), (1 if s > 0 else -1)
        first = (rm if sc > 0 else -rm) - imm if ss > 0 else (rm if sc > 0 else -rm) + imm
        second = (imm if sc > 0 else -imm) + rm if ss > 0 else (imm if sc > 0 else -imm) - rm
        return first, second
    return re * c - im * s, re * s + im * c


def complex_fft(values, sign):
    n = len(values)
    if n == 1:
        return values
    even = complex_fft(values[0::2], sign)
    odd = complex_fft(values[1::2], sign)
    outs = [None] * n
    for k in range(n // 2):
        re, im = times_root(odd[k][0], odd[k][1], k, n, sign)
        outs[k] = (even[k][0] + re, even[k][1] + im)
        outs[k + n // 2] = (even[k][0] - re, even[k][1] - im)
    return outs


def real_fft(values):
    n = len(values)
    if n == 2:
        return [(values[0] + values[1], None), (values[0] - values[1], None)]
    even, odd = real_fft(values[0::2]), real_fft(values[1::2])
    half = n // 2
    outs = [None] * (half + 1)
    outs[0] = (even[0][0] + odd[0][0], None)
    outs[half] = (even[0][0] - odd[0][0], None)
    for k in range(1, half // 2 + 1):
        if 4 * k == n:
            outs[k] = (even[k][0], -odd[k][0])
            continue
        re, im = times_root(odd[k][0], odd[k][1], k, n, -1)
        outs[k] = (even[k][0] + re, even[k][1] + im)
        outs[half - k] = (even[k][0] - re, im - even[k][1])
    return outs


def real_inverse(values):
    half = len(values) - 1
    n = 2 * half
    if n == 2:
        return [values[0][0] + values[1][0], values[0][0] - values[1][0]]
    even, odd = [None] * (half // 2 + 1), [None] * (half // 2 + 1)
    even[0] = (values[0][0] + values[half][0], None)
    odd[0] = (values[0][0] - values[half][0], None)
    for k in range(1, half // 2 + 1):
        if 4 * k == n:
            even[k] = (values[k][0] * 2.0, None)
            odd[k] = (values[k][1] * -2.0, None)
            continue
        (ar, ai), (br, bi) = values[k], values[half - k]
        even[k] = (ar + br, ai - bi)
        odd[k] = times_root(ar - br, ai + bi, k, n, 1)
    low, high = real_inverse(even), real_inverse(odd)
    outs = [None] * n
    outs[0::2] = low
    outs[1::2] = high
    return outs


def split(values):
    high = values.astype(BF16)
    return high, (values - high.astype(F32)).astype(BF16)


def dot(a, b):
    return jnp.dot(a, b, preferred_element_type=F32)


def table_times(high, low, values):
    vh, vl = split(values)
    return dot(high, vh) + (dot(low, vh) + dot(high, vl))


def times_table(values, high, low):
    vh, vl = split(values)
    return dot(vh, high) + (dot(vh, low) + dot(vl, high))


def loop(count, step, unroll=4):
    lax.fori_loop(0, count, lambda i, c: (step(i), c)[1], 0, unroll=unroll)


def tile(t, base=0):
    return pl.ds(pl.multiple_of(base + t * 8, 8), 8)


def chunk(g, c):
    return pl.ds(pl.multiple_of(FIRST_ROW[g] + c * CHUNK[g], 8), CHUNK[g])


def tile_rows(k, j):
    g = 0 if j in GROUPS[0] else 1
    start = FIRST_ROW[g] + GROUPS[g].index(j) * 8
    if isinstance(k, int):
        return pl.ds(start + k * ROWS_OF[g], 8)
    return pl.ds(pl.multiple_of(start + k * ROWS_OF[g], 8), 8)


def row_short_forward(t, tiles, scratch):
    spectrum = real_fft(tiles)
    scratch[0, tile(t), :] = spectrum[0][0]
    scratch[0, tile(t, LANES), :] = spectrum[8][0]
    for j in range(1, 8):
        scratch[j, tile(t), :] = spectrum[j][0]
        scratch[j, tile(t, LANES), :] = spectrum[j][1]


def row_long_forward(g, mat, scratch, out):
    def step(i):
        j = i + GROUP_J[g]
        result = table_times(mat[0, j], mat[1, j], scratch[j])
        out[:, j] = result.reshape(16, 2, 8, LANES)

    loop(4, step)


def row_long_inverse(g, load, mat, scratch):
    def step(i):
        j = i + GROUP_J[g]
        scratch[j] = table_times(mat[0, j], mat[1, j], load(j))

    loop(4, step)


def row_short_inverse(t, scratch):
    spectrum = [(scratch[0, tile(t), :], None)]
    spectrum += [(scratch[j, tile(t), :], scratch[j, tile(t, LANES), :]) for j in range(1, 8)]
    spectrum.append((scratch[0, tile(t, LANES), :], None))
    return real_inverse(spectrum)


def col_forward(g, received, first_mask, mats, twiddle, scratch, emit):
    def transform(values, start):
        spectrum = complex_fft(values, -1)
        for k in range(16):
            re, im = spectrum[k]
            if k:
                c, s = twiddle[k, 0], twiddle[k, 1]
                re, im = re * c + im * s, im * c - re * s
            rows = pl.ds(start + k * ROWS_OF[g], 8)
            scratch[rows, 0:LANES] = re
            scratch[rows, LANES : 2 * LANES] = im

    for n, j in enumerate(GROUPS[g]):
        start = FIRST_ROW[g] + n * 8
        if j == 0:
            values = [
                (received[b, 0, 0], jnp.where(first_mask, 0.0, received[b, 0, 1])) for b in range(16)
            ]
        elif j == 8:
            zero = jnp.zeros((8, LANES), F32)
            values = [(jnp.where(first_mask, received[b, 0, 1], 0.0), zero) for b in range(16)]
        else:
            values = [(received[b, j, 0], received[b, j, 1]) for b in range(16)]
        transform(values, start)

    def step(c):
        rows = chunk(g, c)
        emit(rows, c, times_table(scratch[rows, :], mats[0, 0], mats[0, 1]))

    loop(4, step)


def col_inverse(g, load, first_mask, mats, twiddle, scratch, out):
    def step(c):
        rows = chunk(g, c)
        scratch[rows, :] = times_table(load(rows), mats[1, 0], mats[1, 1])

    loop(4, step)

    def transform(n):
        values = []
        for k in range(16):
            rows = pl.ds(FIRST_ROW[g] + n * 8 + k * ROWS_OF[g], 8)
            re = scratch[rows, 0:LANES]
            im = scratch[rows, LANES : 2 * LANES]
            if k:
                c, s = twiddle[k, 0], twiddle[k, 1]
                re, im = re * c - im * s, im * c + re * s
            values.append((re, im))
        return complex_fft(values, 1)

    if g == 0:
        for b, (re, im) in enumerate(transform(1)):
            out[b, 0, 0] = re
        for b, (re, im) in enumerate(transform(0)):
            out[b, 0, 1] = jnp.where(first_mask, out[b, 0, 0], im)
            out[b, 0, 0] = re
    for n, j in enumerate(GROUPS[g]):
        if j not in (0, 8):
            for b, (re, im) in enumerate(transform(n)):
                out[b, j, 0] = re
                out[b, j, 1] = im


def partners(me):
    core = me % 2
    step = [(1 - 2 * ((me // (1 << k)) % 2)) * (1 << k) for k in range(4)]

    def other(offset):
        return me + sum(step[k] for k in range(4) if (offset >> k) & 1)

    return [other(i) * (1 - core) + other(16 - i) * core for i in range(1, 16)]


def kernel(
    vort, row_hbm, col_mats, twiddle, flips, waves,
    grad, resid,
    rowm, grid_a, grid_u, grid_v, grid_wx, grid_wy, sends, recvs, local_b,
    row_s, col_s, w_spec, e_spec, adj, next_start, prev_end,
    dx_t, linv_t, decay_t, nlf_t, flat, grad_v, resid_v,
    table_sem, out_sem, own_sem, send_sem, recv_sem, seg_send, seg_recv,
):
    me = lax.axis_index("space")
    seg = lax.axis_index("seg")
    after, before = (seg + 1) % 8, (seg + 7) % 8
    rows_in_tile = lax.broadcasted_iota(jnp.int32, (8, LANES), 0)
    first_mask = (rows_in_tile == 0) & (jnp.zeros((8, LANES), jnp.int32) + me == 0)
    others = partners(me)
    both = (0, 1)

    def table_copy(i):
        return pltpu.make_async_copy(row_hbm.at[i], rowm.at[i], table_sem.at[i])

    for i in (0, 3, 2, 1):
        table_copy(i).start()

    barrier = pltpu.get_barrier_semaphore()
    for p in others:
        pl.semaphore_signal(barrier, inc=1, device_id={"space": p}, device_id_type=MESH)
    for s in (after, before):
        for p in others + [me]:
            pl.semaphore_signal(
                barrier, inc=1, device_id={"seg": s, "space": p}, device_id_type=MESH)

    def part(f, g, p):
        return (f, p, pl.ds(GROUP_J[g], 4))

    def own_copy(f, g):
        return pltpu.make_async_copy(
            sends.at[part(f, g, me)], recvs.at[part(f, g, me)], own_sem.at[f, g])

    def start(f, g):
        own_copy(f, g).start()

        def one(p):
            pltpu.make_async_remote_copy(
                src_ref=sends.at[part(f, g, p)], dst_ref=recvs.at[part(f, g, me)],
                send_sem=send_sem.at[f, g], recv_sem=recv_sem.at[f, g],
                device_id={"space": p}, device_id_type=MESH).start()

        if f == 4:
            for p in others:
                pl.when(p < KEPT)(functools.partial(one, p))
        elif f == 5:
            @pl.when(me < KEPT)
            def _():
                for p in others:
                    one(p)
        else:
            for p in others:
                one(p)

    def wait_bytes(f, g, sem, count):
        pltpu.make_async_copy(
            sends.at[part(f, g, pl.ds(0, count))], recvs.at[part(f, g, pl.ds(0, count))],
            sem.at[f, g]).wait()

    def some(f, g, sem):
        @pl.when(me < KEPT)
        def _():
            wait_bytes(f, g, sem, KEPT - 1)

        @pl.when(me >= KEPT)
        def _():
            wait_bytes(f, g, sem, KEPT)

    def inside(f, g, sem):
        @pl.when(me < KEPT)
        def _():
            wait_bytes(f, g, sem, 15)

    def finish(f, g):
        own_copy(f, g).wait()
        kind = {4: inside, 5: some}.get(f)
        if kind:
            kind(f, g, recv_sem)
        else:
            wait_bytes(f, g, recv_sem, 15)

    def finish_send(f, g):
        kind = {4: some, 5: inside}.get(f)
        if kind:
            kind(f, g, send_sem)
        else:
            wait_bytes(f, g, send_sem, 15)

    def start_before():
        for p in [me] + others:
            pltpu.make_async_remote_copy(
                src_ref=sends.at[0, p], dst_ref=recvs.at[10, me],
                send_sem=send_sem.at[10, 0], recv_sem=recv_sem.at[10, 0],
                device_id={"seg": before, "space": p}, device_id_type=MESH).start()

    def wait_before(sem):
        pltpu.make_async_copy(sends.at[0], recvs.at[10], sem.at[10, 0]).wait()

    def seg_copy():
        return pltpu.make_async_remote_copy(
            src_ref=e_spec, dst_ref=prev_end, send_sem=seg_send, recv_sem=seg_recv,
            device_id={"seg": after}, device_id_type=MESH)

    for b in range(16):
        grid_a[b] = vort[:, b * LANES : (b + 1) * LANES].T

    def tiles_of(ref, t):
        return [ref[b, tile(t), :] for b in range(16)]

    def keep(ref, t, tiles):
        for b in range(16):
            ref[b, tile(t), :] = tiles[b]

    loop(16, lambda t: row_short_forward(t, tiles_of(grid_a, t), row_s.at[0]))
    table_copy(0).wait()
    for g in both:
        row_long_forward(g, rowm.at[0], row_s.at[0], sends.at[0])
        if g == 0:
            pl.semaphore_wait(barrier, 47)
        start(0, g)

    def stacked(f):
        return lambda j: sends[f, :, j].reshape(256, LANES)

    def arrived(f):
        return lambda j: recvs[f, :, j].reshape(256, LANES)

    for g in both:
        first = 0 if g == 0 else CHUNK[0]
        ky = waves[0, first : first + CHUNK[g], :] + waves[1, first : first + CHUNK[g], :] * me.astype(F32)

        def make_tables(c, g=g, ky=ky):
            rows = lax.broadcasted_iota(jnp.int32, (CHUNK[g], LANES), 0)
            lanes = lax.broadcasted_iota(jnp.int32, (CHUNK[g], LANES), 1)
            k = 4 * c + 16 * lanes
            for q in range(1, 4):
                k = k + jnp.where(rows >= q * ROWS_OF[g], 1, 0)
            kx = jnp.where(k < N // 2, k, k - N)
            kxf = kx.astype(F32)
            square = kxf * kxf + ky * ky
            decay = jnp.exp(-TIME_STEP * (DRAG + 9.0 * square / (N * N)))
            to = chunk(g, c)
            dx_t[to, :] = jnp.where(kx == -(N // 2), 0.0, kxf)
            linv_t[to, :] = jnp.where(square > 0.0, 1.0 / jnp.maximum(square, 1.0), 0.0)
            decay_t[to, :] = decay
            keep_mask = (3.0 * jnp.abs(kxf) <= N) & (3.0 * jnp.abs(ky) <= N)
            nlf_t[to, :] = jnp.where(keep_mask, TIME_STEP * decay, 0.0)

        loop(4, make_tables, 1)

    def zero_columns(b):
        recvs[5, b] = jnp.zeros((8, 2, 8, LANES), F32)

    @pl.when(me >= KEPT)
    def _():
        loop(16, lambda b: recvs.__setitem__((4, b), jnp.zeros((8, 2, 8, LANES), F32)), 1)

    loop(16 - KEPT, lambda b: zero_columns(b + KEPT), 1)
    flat[...] = jnp.zeros_like(flat)

    def two(re, im):
        return jnp.concatenate([re, im], axis=1)

    def halves(ref, rows):
        return ref[rows, 0:LANES], ref[rows, LANES : 2 * LANES]

    def psi_hat(rows):
        re, im = halves(w_spec, rows)
        linv = linv_t[rows, :]
        return two(linv * re, linv * im)

    def v_hat(rows):
        re, im = halves(w_spec, rows)
        factor = linv_t[rows, :] * dx_t[rows, :]
        return two(factor * im, -factor * re)

    def wx_hat(rows):
        re, im = halves(w_spec, rows)
        factor = dx_t[rows, :]
        return two(-factor * im, factor * re)

    def forward_columns(g, f, emit):
        col_forward(g, recvs.at[f], first_mask, col_mats, twiddle, col_s, emit)

    def inverse_columns(g, f, load):
        col_inverse(g, load, first_mask, col_mats, twiddle, col_s, sends.at[f])
        start(f, g)

    def put(ref):
        def emit(rows, c, value):
            ref[rows, :] = value
        return emit

    for g in both:
        finish(0, g)
        forward_columns(g, 0, put(w_spec))
        inverse_columns(g, 1, psi_hat)
        inverse_columns(g, 2, v_hat)
        inverse_columns(g, 3, wx_hat)
    start_before()

    table_copy(3).wait()
    for g in both:
        row_long_inverse(g, stacked(0), rowm.at[3], row_s.at[0])
    loop(16, lambda t: keep(grid_wy, t, row_short_inverse(t, row_s.at[0])))
    table_copy(2).wait()

    for g in both:
        finish(1, g)
        row_long_inverse(g, arrived(1), rowm.at[3], row_s.at[0])
        if g == 1:
            loop(16, lambda t: keep(grid_u, t, row_short_inverse(t, row_s.at[0])))
        finish(2, g)
        row_long_inverse(g, arrived(2), rowm.at[2], row_s.at[1])
        if g == 1:
            loop(16, lambda t: keep(grid_v, t, row_short_inverse(t, row_s.at[1])))
        finish(3, g)
        row_long_inverse(g, arrived(3), rowm.at[2], row_s.at[2])

    def nonlinear(t):
        tiles = row_short_inverse(t, row_s.at[2])
        product = []
        for b in range(16):
            grid_wx[b, tile(t), :] = tiles[b]
            product.append(
                grid_u[b, tile(t), :] * tiles[b] + grid_v[b, tile(t), :] * grid_wy[b, tile(t), :])
        row_short_forward(t, product, row_s.at[0])

    loop(16, nonlinear)
    for g in both:
        row_long_forward(g, rowm.at[0], row_s.at[0], sends.at[4])
        start(4, g)
    table_copy(1).wait()

    wait_before(recv_sem)
    for g in both:
        forward_columns(g, 10, put(next_start))

    for g in both:
        first = 0 if g == 0 else CHUNK[0]
        ky = waves[0, first : first + CHUNK[g], :] + waves[1, first : first + CHUNK[g], :] * me.astype(F32)

        def put_end(rows, c, value, ky=ky):
            re, im = halves(w_spec, rows)
            decay, nlf, dx = decay_t[rows, :], nlf_t[rows, :], dx_t[rows, :]
            forced = (dx == 0.0) & (nlf > 0.0) & (ky == float(FORCING_WAVE))
            force = jnp.where(forced, TIME_STEP * FORCE_AMP * (N * N / 2.0) * decay, 0.0)
            end_re = decay * re - nlf * value[:, 0:LANES] + force
            end_im = decay * im - nlf * value[:, LANES : 2 * LANES]
            e_spec[rows, :] = two(end_re, end_im)
            next_re, next_im = halves(next_start, rows)
            adj[rows, :] = two(end_re - next_re, end_im - next_im)

        def weight_hat(rows):
            re, im = halves(adj, rows)
            nlf = nlf_t[rows, :]
            return two(nlf * re, nlf * im)

        finish(4, g)
        forward_columns(g, 4, put_end)
        inverse_columns(g, 5, weight_hat)
    seg_copy().start()

    for g in both:
        finish(5, g)
        row_long_inverse(g, arrived(5), rowm.at[2], row_s.at[0])

    def weighted(t):
        tiles = row_short_inverse(t, row_s.at[0])
        keep(grid_a, t, tiles)
        row_short_forward(t, [tiles[b] * grid_u[b, tile(t), :] for b in range(16)], row_s.at[1])

    def product(ref, scratch):
        def step(t):
            tiles = [grid_a[b, tile(t), :] * ref[b, tile(t), :] for b in range(16)]
            row_short_forward(t, tiles, scratch)
        return step

    loop(16, weighted)
    for g in both:
        row_long_forward(g, rowm.at[0], row_s.at[1], sends.at[6])
        start(6, g)
    for f, ref, mat in ((7, grid_wx, 1), (8, grid_wy, 0)):
        loop(16, product(ref, row_s.at[0]))
        for g in both:
            row_long_forward(g, rowm.at[mat], row_s.at[0], sends.at[f])
            start(f, g)
    loop(16, product(grid_v, row_s.at[0]))
    for g in both:
        row_long_forward(g, rowm.at[1], row_s.at[0], local_b)

    seg_copy().wait_recv()

    def make_residual(g):
        def step(c):
            rows = chunk(g, c)
            prev_re, prev_im = halves(prev_end, rows)
            re, im = halves(w_spec, rows)
            res_re, res_im = prev_re - re, prev_im - im
            prev_end[rows, :] = two(res_re, res_im)
            adj_re, adj_im = halves(adj, rows)
            decay = decay_t[rows, :]
            adj[rows, :] = two(decay * adj_re - res_re, decay * adj_im - res_im)
        return step

    for g in both:
        loop(4, make_residual(g), 1)

    slots = slot_table()

    def write_residual(k, mirror, flip):
        for part in range(2):
            lanes = slice(part * LANES, (part + 1) * LANES)
            for j in range(8):
                direct = prev_end[tile_rows(k, j), lanes]
                mirrored = prev_end[tile_rows(mirror, j), lanes]
                if part:
                    mirrored = -mirrored
                for h in range(2):
                    to = int(slots[j, 4 * h])
                    flat[part, 0, pl.ds(to, 4, stride=16), :] = direct[4 * h : 4 * h + 4]
                    flat[part, 1, pl.ds(64 + to, 4, stride=16), :] = mirrored[4 * h : 4 * h + 4]
            extra = prev_end[tile_rows(k, 8), lanes]
            flat[part, 0, 64:72, :] = jnp.where(first_mask, extra, 0.0)
            flat[part, 1, 64:72, :] = jnp.where(first_mask, 0.0, flat[part, 1, 64:72, :])
            high, low = split(jnp.concatenate([flat[part, 0], flat[part, 1]], axis=1))
            contract = (((1,), (1,)), ((), ()))
            result = lax.dot_general(flip, high, contract, preferred_element_type=F32)
            result = result + lax.dot_general(flip, low, contract, preferred_element_type=F32)
            resid_v[part, :, k, :] = result

    write_residual(0, 0, flips[0])
    loop(15, lambda i: write_residual(i + 1, 15 - i, flips[1]), 1)
    resid_copy = pltpu.make_async_copy(resid_v, resid, out_sem.at[0])
    resid_copy.start()

    def add_a(rows, c, value):
        re, im = halves(adj, rows)
        dx = dx_t[rows, :]
        adj[rows, :] = two(re - dx * value[:, LANES : 2 * LANES], im + dx * value[:, 0:LANES])

    def add_c(rows, c, value):
        re, im = halves(adj, rows)
        linv = linv_t[rows, :]
        adj[rows, :] = two(re + linv * value[:, 0:LANES], im + linv * value[:, LANES : 2 * LANES])

    def add_d(rows, c, value):
        re, im = halves(adj, rows)
        factor = linv_t[rows, :] * dx_t[rows, :]
        adj[rows, :] = two(
            re + factor * value[:, LANES : 2 * LANES], im - factor * value[:, 0:LANES])

    for f, emit in ((6, add_a), (7, add_c), (8, add_d)):
        for g in both:
            finish(f, g)
            forward_columns(g, f, emit)
            if f == 8:
                inverse_columns(g, 9, lambda rows: adj[rows, :])

    def total(j):
        return (recvs[9, :, j] + local_b[:, j]).reshape(256, LANES)

    for g in both:
        finish(9, g)
        row_long_inverse(g, total, rowm.at[2], row_s.at[0])
    loop(16, lambda t: keep(grid_a, t, row_short_inverse(t, row_s.at[0])))
    for b in range(16):
        grad_v[:, b * LANES : (b + 1) * LANES] = grid_a[b].T
    grad_copy = pltpu.make_async_copy(grad_v, grad, out_sem.at[1])
    grad_copy.start()
    for f in range(10):
        for g in both:
            finish_send(f, g)
    wait_before(send_sem)
    seg_copy().wait_send()
    resid_copy.wait()
    grad_copy.wait()


def body(vorticity):
    col_mats, twiddle = col_tables()
    vmem = pl.BlockSpec(memory_space=pltpu.VMEM)
    hbm = pl.BlockSpec(memory_space=pl.ANY)
    slab = (16, 8, 2, 8, LANES)
    grid = pltpu.VMEM((16, LANES, LANES), F32)
    spectrum = pltpu.VMEM((ALL_ROWS, 2 * LANES), F32)
    factor = pltpu.VMEM((ALL_ROWS, LANES), F32)
    outs = ((LANES, N), (2, LANES, 16, LANES))
    gradient, residual = pl.pallas_call(
        kernel,
        out_shape=tuple(jax.ShapeDtypeStruct(shape, F32) for shape in outs),
        in_specs=[vmem, hbm, vmem, vmem, vmem, vmem],
        out_specs=(hbm, hbm),
        scratch_shapes=[
            pltpu.VMEM((4, 2, 8, 256, 256), BF16),
            grid, grid, grid, grid, grid,
            pltpu.VMEM((10,) + slab, F32),
            pltpu.VMEM((11,) + slab, F32),
            pltpu.VMEM(slab, F32),
            pltpu.VMEM((3, 8, 256, LANES), F32),
            spectrum, spectrum, spectrum, spectrum, spectrum, spectrum,
            factor, factor, factor, factor,
            pltpu.VMEM((2, 2, LANES, LANES), F32),
            pltpu.VMEM(outs[0], F32),
            pltpu.VMEM(outs[1], F32),
            pltpu.SemaphoreType.DMA((4,)),
            pltpu.SemaphoreType.DMA((2,)),
            pltpu.SemaphoreType.DMA((10, 2)),
            pltpu.SemaphoreType.DMA((11, 2)),
            pltpu.SemaphoreType.DMA((11, 2)),
            pltpu.SemaphoreType.DMA,
            pltpu.SemaphoreType.DMA,
        ],
        compiler_params=pltpu.CompilerParams(
            collective_id=0, has_side_effects=True, vmem_limit_bytes=62 * 2**20
        ),
        name="orbit_gradient",
    )(vorticity[0], jnp.asarray(row_tables()), jnp.asarray(col_mats), jnp.asarray(twiddle),
      jnp.asarray(flip_tables()), jnp.asarray(wave_table()))
    return gradient[None], residual.reshape(1, 2, N, LANES)


def solution(mesh):
    return jax.shard_map(
        body,
        mesh=mesh,
        in_specs=(P("seg", "space", None),),
        out_specs=(P("seg", "space", None), P("seg", None, None, "space")),
        check_vma=False,
    )
```

```python
import functools
import math

import jax
import jax.numpy as jnp
import ml_dtypes
import numpy as np
from jax import lax
from jax.experimental import pallas as pl
from jax.experimental.pallas import tpu as pltpu
from jax.sharding import PartitionSpec as P

N = 2048
SLABS = 16
LANES = 128
GROUPS = ((0, 8, 1, 2, 3), (4, 5, 6, 7))
GROUP_J = (0, 4)
ROWS_OF = (40, 32)
FIRST_ROW = (0, 640)
CHUNK = (160, 128)
ALL_ROWS = 16 * (40 + 32)
KEPT = 11
TIME_STEP = 0.3
DRAG = 0.05
FORCE_AMP = 0.8
FORCING_WAVE = 4
MESH = pl.DeviceIdType.MESH
F32 = jnp.float32
BF16 = jnp.bfloat16


def split_table(table):
    high = table.astype(np.float32).astype(ml_dtypes.bfloat16)
    low = (table - high.astype(np.float64)).astype(np.float32).astype(ml_dtypes.bfloat16)
    return high, low


def slot_wave(j, d, r):
    if r < 4:
        return j + 16 * (4 * d + r)
    return (16 - j if j else 8) + 16 * (4 * d + r - 4)


@functools.cache
def row_tables():
    a = np.arange(LANES)
    forward = np.zeros((8, 16, 2, 8, 2, LANES))
    inverse = np.zeros((8, 2, LANES, 16, 2, 8))
    wave = np.zeros((8, 16, 8))
    for j in range(8):
        for d in range(16):
            for r in range(8):
                k = slot_wave(j, d, r)
                wave[j, d, r] = k
                c = np.cos(2 * np.pi * ((a * k) % N) / N)
                s = np.sin(2 * np.pi * ((a * k) % N) / N)
                if j == 0:
                    part = 0 if r < 4 else 1
                    forward[j, d, 0, r, part] = c
                    forward[j, d, 1, r, part] = -s
                    inverse[j, part, :, d, 0, r] = 2 * c
                    inverse[j, part, :, d, 1, r] = -2 * s
                    if k == 0:
                        alternate = 1.0 - 2.0 * (a % 2)
                        forward[j, d, 1, r, part] = alternate
                        inverse[j, part, :, d, 0, r] = 1.0
                        inverse[j, part, :, d, 1, r] = alternate
                else:
                    sign = 1.0 if r < 4 else -1.0
                    forward[j, d, 0, r, 0] = c
                    forward[j, d, 0, r, 1] = sign * s
                    forward[j, d, 1, r, 0] = -s
                    forward[j, d, 1, r, 1] = sign * c
                    inverse[j, 0, :, d, 0, r] = c
                    inverse[j, 0, :, d, 1, r] = -s
                    inverse[j, 1, :, d, 0, r] = sign * s
                    inverse[j, 1, :, d, 1, r] = sign * c
    inverse /= N
    dwave = wave[:, :, None, :, None, None]
    forward_dy = np.stack([-forward[:, :, 1], forward[:, :, 0]], axis=2) * dwave
    inverse_dy = np.stack([inverse[..., 1, :], -inverse[..., 0, :]], axis=-2) * wave[:, None, None, :, None, :]
    shape = (8, 256, 256)
    outs = []
    for table in (forward, forward_dy, inverse, inverse_dy):
        high, low = split_table(table.reshape(shape))
        outs.append(np.stack([high, low]))
    return np.stack(outs)


@functools.cache
def col_tables():
    a = np.arange(LANES)
    angle = 2 * np.pi * (np.outer(a, a) % LANES) / LANES
    c, s = np.cos(angle), np.sin(angle)
    forward = np.block([[c, -s], [s, c]])
    inverse = np.block([[c, s], [-s, c]]) / N
    mats = np.stack([np.stack(split_table(m)) for m in (forward, inverse)])
    angle = 2 * np.pi * np.outer(np.arange(16), a) / N
    twiddle = np.stack([np.cos(angle), np.sin(angle)], axis=1)
    twiddle = np.broadcast_to(twiddle[:, :, None, :], (16, 2, 8, LANES)).astype(np.float32)
    return mats, np.ascontiguousarray(twiddle)


@functools.cache
def flip_tables():
    eye = np.eye(LANES)
    first = np.concatenate([eye, eye[(LANES - np.arange(LANES)) % LANES]], axis=1)
    other = np.concatenate([eye, eye[LANES - 1 - np.arange(LANES)]], axis=1)
    return (np.stack([first, other]) / N).astype(ml_dtypes.bfloat16)


@functools.cache
def slot_table():
    return np.array([[slot_wave(j, 0, r) for r in range(8)] for j in range(8)], np.int32)


@functools.cache
def wave_table():
    table = np.zeros((2, CHUNK[0] + CHUNK[1], LANES), np.float32)
    row = 0
    for group in GROUPS:
        for _ in range(4):
            for j in group:
                table[0, row : row + 8] = (N // 2) if j == 8 else slot_table()[j][:, None]
                table[1, row : row + 8] = 0 if j == 8 else 64
                row += 8
    return table


def times_root(re, im, k, n, sign):
    k = k % n
    if im is None:
        if k == 0:
            return re, None
        angle = sign * 2 * math.pi * k / n
        if 4 * k == n:
            return None, (re if sign > 0 else -re)
        return re * math.cos(angle), re * math.sin(angle)
    if k == 0:
        return re, im
    if 2 * k == n:
        return -re, -im
    if 4 * k == n:
        return (-im, re) if sign > 0 else (im, -re)
    if 4 * k == 3 * n:
        return (im, -re) if sign > 0 else (-im, re)
    angle = sign * 2 * math.pi * k / n
    c, s = math.cos(angle), math.sin(angle)
    if 8 * k == n or 8 * k == 3 * n or 8 * k == 5 * n or 8 * k == 7 * n:
        m = abs(c)
        rm, imm = re * m, im * m
        sc, ss = (1 if c > 0 else -1), (1 if s > 0 else -1)
        first = (rm if sc > 0 else -rm) - imm if ss > 0 else (rm if sc > 0 else -rm) + imm
        second = (imm if sc > 0 else -imm) + rm if ss > 0 else (imm if sc > 0 else -imm) - rm
        return first, second
    return re * c - im * s, re * s + im * c


def complex_fft(values, sign):
    n = len(values)
    if n == 1:
        return values
    even = complex_fft(values[0::2], sign)
    odd = complex_fft(values[1::2], sign)
    outs = [None] * n
    for k in range(n // 2):
        re, im = times_root(odd[k][0], odd[k][1], k, n, sign)
        outs[k] = (even[k][0] + re, even[k][1] + im)
        outs[k + n // 2] = (even[k][0] - re, even[k][1] - im)
    return outs


def real_fft(values):
    n = len(values)
    if n == 2:
        return [(values[0] + values[1], None), (values[0] - values[1], None)]
    even, odd = real_fft(values[0::2]), real_fft(values[1::2])
    half = n // 2
    outs = [None] * (half + 1)
    outs[0] = (even[0][0] + odd[0][0], None)
    outs[half] = (even[0][0] - odd[0][0], None)
    for k in range(1, half // 2 + 1):
        if 4 * k == n:
            outs[k] = (even[k][0], -odd[k][0])
            continue
        re, im = times_root(odd[k][0], odd[k][1], k, n, -1)
        outs[k] = (even[k][0] + re, even[k][1] + im)
        outs[half - k] = (even[k][0] - re, im - even[k][1])
    return outs


def real_inverse(values):
    half = len(values) - 1
    n = 2 * half
    if n == 2:
        return [values[0][0] + values[1][0], values[0][0] - values[1][0]]
    even, odd = [None] * (half // 2 + 1), [None] * (half // 2 + 1)
    even[0] = (values[0][0] + values[half][0], None)
    odd[0] = (values[0][0] - values[half][0], None)
    for k in range(1, half // 2 + 1):
        if 4 * k == n:
            even[k] = (values[k][0] * 2.0, None)
            odd[k] = (values[k][1] * -2.0, None)
            continue
        (ar, ai), (br, bi) = values[k], values[half - k]
        even[k] = (ar + br, ai - bi)
        odd[k] = times_root(ar - br, ai + bi, k, n, 1)
    low, high = real_inverse(even), real_inverse(odd)
    outs = [None] * n
    outs[0::2] = low
    outs[1::2] = high
    return outs


def split(values):
    high = values.astype(BF16)
    return high, (values - high.astype(F32)).astype(BF16)


def dot(a, b):
    return jnp.dot(a, b, preferred_element_type=F32)


def table_times(high, low, values):
    vh, vl = split(values)
    return dot(high, vh) + (dot(low, vh) + dot(high, vl))


def times_table(values, high, low):
    vh, vl = split(values)
    return dot(vh, high) + (dot(vh, low) + dot(vl, high))


def loop(count, step, unroll=4):
    lax.fori_loop(0, count, lambda i, c: (step(i), c)[1], 0, unroll=unroll)


def tile(t, base=0):
    return pl.ds(pl.multiple_of(base + t * 8, 8), 8)


def chunk(g, c):
    return pl.ds(pl.multiple_of(FIRST_ROW[g] + c * CHUNK[g], 8), CHUNK[g])


def tile_rows(k, j):
    g = 0 if j in GROUPS[0] else 1
    start = FIRST_ROW[g] + GROUPS[g].index(j) * 8
    if isinstance(k, int):
        return pl.ds(start + k * ROWS_OF[g], 8)
    return pl.ds(pl.multiple_of(start + k * ROWS_OF[g], 8), 8)


def row_short_forward(t, tiles, scratch):
    spectrum = real_fft(tiles)
    scratch[0, tile(t), :] = spectrum[0][0]
    scratch[0, tile(t, LANES), :] = spectrum[8][0]
    for j in range(1, 8):
        scratch[j, tile(t), :] = spectrum[j][0]
        scratch[j, tile(t, LANES), :] = spectrum[j][1]


def row_long_forward(g, mat, scratch, out):
    def step(i):
        j = i + GROUP_J[g]
        result = table_times(mat[0, j], mat[1, j], scratch[j])
        out[:, j] = result.reshape(16, 2, 8, LANES)

    loop(4, step)


def row_long_inverse(g, load, mat, scratch):
    def step(i):
        j = i + GROUP_J[g]
        scratch[j] = table_times(mat[0, j], mat[1, j], load(j))

    loop(4, step)


def row_short_inverse(t, scratch):
    spectrum = [(scratch[0, tile(t), :], None)]
    spectrum += [(scratch[j, tile(t), :], scratch[j, tile(t, LANES), :]) for j in range(1, 8)]
    spectrum.append((scratch[0, tile(t, LANES), :], None))
    return real_inverse(spectrum)


def col_forward(g, received, first_mask, mats, twiddle, scratch, emit):
    def transform(values, start):
        spectrum = complex_fft(values, -1)
        for k in range(16):
            re, im = spectrum[k]
            if k:
                c, s = twiddle[k, 0], twiddle[k, 1]
                re, im = re * c + im * s, im * c - re * s
            rows = pl.ds(start + k * ROWS_OF[g], 8)
            scratch[rows, 0:LANES] = re
            scratch[rows, LANES : 2 * LANES] = im

    for n, j in enumerate(GROUPS[g]):
        start = FIRST_ROW[g] + n * 8
        if j == 0:
            values = [
                (received[b, 0, 0], jnp.where(first_mask, 0.0, received[b, 0, 1])) for b in range(16)
            ]
        elif j == 8:
            zero = jnp.zeros((8, LANES), F32)
            values = [(jnp.where(first_mask, received[b, 0, 1], 0.0), zero) for b in range(16)]
        else:
            values = [(received[b, j, 0], received[b, j, 1]) for b in range(16)]
        transform(values, start)

    def step(c):
        rows = chunk(g, c)
        emit(rows, c, times_table(scratch[rows, :], mats[0, 0], mats[0, 1]))

    loop(4, step)


def col_inverse(g, load, first_mask, mats, twiddle, scratch, out):
    def step(c):
        rows = chunk(g, c)
        scratch[rows, :] = times_table(load(rows), mats[1, 0], mats[1, 1])

    loop(4, step)

    def transform(n):
        values = []
        for k in range(16):
            rows = pl.ds(FIRST_ROW[g] + n * 8 + k * ROWS_OF[g], 8)
            re = scratch[rows, 0:LANES]
            im = scratch[rows, LANES : 2 * LANES]
            if k:
                c, s = twiddle[k, 0], twiddle[k, 1]
                re, im = re * c - im * s, im * c + re * s
            values.append((re, im))
        return complex_fft(values, 1)

    if g == 0:
        for b, (re, im) in enumerate(transform(1)):
            out[b, 0, 0] = re
        for b, (re, im) in enumerate(transform(0)):
            out[b, 0, 1] = jnp.where(first_mask, out[b, 0, 0], im)
            out[b, 0, 0] = re
    for n, j in enumerate(GROUPS[g]):
        if j not in (0, 8):
            for b, (re, im) in enumerate(transform(n)):
                out[b, j, 0] = re
                out[b, j, 1] = im


def partners(me):
    core = me % 2
    step = [(1 - 2 * ((me // (1 << k)) % 2)) * (1 << k) for k in range(4)]

    def other(offset):
        return me + sum(step[k] for k in range(4) if (offset >> k) & 1)

    return [other(i) * (1 - core) + other(16 - i) * core for i in range(1, 16)]


def kernel(
    vort, row_hbm, col_mats, twiddle, flips, waves,
    grad, resid,
    rowm, grid_a, grid_u, grid_v, grid_wx, grid_wy, sends, recvs, local_b,
    row_s, col_s, w_spec, previous, adj, next_start, residual,
    dx_t, linv_t, decay_t, nlf_t, flat, grad_v, resid_v,
    table_sem, out_sem, own_sem, send_sem, recv_sem,
):
    me = lax.axis_index("space")
    seg = lax.axis_index("seg")
    after, before = (seg + 1) % 8, (seg + 7) % 8
    rows_in_tile = lax.broadcasted_iota(jnp.int32, (8, LANES), 0)
    first_mask = (rows_in_tile == 0) & (jnp.zeros((8, LANES), jnp.int32) + me == 0)
    others = partners(me)
    both = (0, 1)

    def table_copy(i):
        return pltpu.make_async_copy(row_hbm.at[i], rowm.at[i], table_sem.at[i])

    for i in (0, 3, 2, 1):
        table_copy(i).start()

    barrier = pltpu.get_barrier_semaphore()
    for p in others:
        pl.semaphore_signal(barrier, inc=1, device_id={"space": p}, device_id_type=MESH)
    for s in (after, before):
        for p in others + [me]:
            pl.semaphore_signal(
                barrier, inc=1, device_id={"seg": s, "space": p}, device_id_type=MESH)

    def part(f, g, p):
        return (f, p, pl.ds(GROUP_J[g], 4))

    def own_copy(f, g):
        return pltpu.make_async_copy(
            sends.at[part(f, g, me)], recvs.at[part(f, g, me)], own_sem.at[f, g])

    def start(f, g):
        own_copy(f, g).start()

        def one(p):
            pltpu.make_async_remote_copy(
                src_ref=sends.at[part(f, g, p)], dst_ref=recvs.at[part(f, g, me)],
                send_sem=send_sem.at[f, g], recv_sem=recv_sem.at[f, g],
                device_id={"space": p}, device_id_type=MESH).start()

        if f == 4:
            for p in others:
                pl.when(p < KEPT)(functools.partial(one, p))
        elif f == 5:
            @pl.when(me < KEPT)
            def _():
                for p in others:
                    one(p)
        else:
            for p in others:
                one(p)

    def wait_bytes(f, g, sem, count):
        pltpu.make_async_copy(
            sends.at[part(f, g, pl.ds(0, count))], recvs.at[part(f, g, pl.ds(0, count))],
            sem.at[f, g]).wait()

    def some(f, g, sem):
        @pl.when(me < KEPT)
        def _():
            wait_bytes(f, g, sem, KEPT - 1)

        @pl.when(me >= KEPT)
        def _():
            wait_bytes(f, g, sem, KEPT)

    def inside(f, g, sem):
        @pl.when(me < KEPT)
        def _():
            wait_bytes(f, g, sem, 15)

    def finish(f, g):
        own_copy(f, g).wait()
        kind = {4: inside, 5: some}.get(f)
        if kind:
            kind(f, g, recv_sem)
        else:
            wait_bytes(f, g, recv_sem, 15)

    def finish_send(f, g):
        kind = {4: some, 5: inside}.get(f)
        if kind:
            kind(f, g, send_sem)
        else:
            wait_bytes(f, g, send_sem, 15)

    side = {10: (0, before), 11: (0, after), 12: (4, after)}

    def start_side(f):
        source, s = side[f]

        def one(p):
            pltpu.make_async_remote_copy(
                src_ref=sends.at[source, p], dst_ref=recvs.at[f, me],
                send_sem=send_sem.at[f, 0], recv_sem=recv_sem.at[f, 0],
                device_id={"seg": s, "space": p}, device_id_type=MESH).start()

        for p in [me] + others:
            if f == 12:
                pl.when(p < KEPT)(functools.partial(one, p))
            else:
                one(p)

    def wait_side(f, sem, count=16):
        pltpu.make_async_copy(
            sends.at[side[f][0], pl.ds(0, count)], recvs.at[f, pl.ds(0, count)], sem.at[f, 0]).wait()

    def finish_side(f):
        if f == 12:
            pl.when(me < KEPT)(lambda: wait_side(f, recv_sem))
        else:
            wait_side(f, recv_sem)

    for b in range(16):
        grid_a[b] = vort[:, b * LANES : (b + 1) * LANES].T

    def tiles_of(ref, t):
        return [ref[b, tile(t), :] for b in range(16)]

    def keep(ref, t, tiles):
        for b in range(16):
            ref[b, tile(t), :] = tiles[b]

    loop(16, lambda t: row_short_forward(t, tiles_of(grid_a, t), row_s.at[0]))
    table_copy(0).wait()
    for g in both:
        row_long_forward(g, rowm.at[0], row_s.at[0], sends.at[0])
        if g == 0:
            pl.semaphore_wait(barrier, 47)
        start(0, g)

    def stacked(f):
        return lambda j: sends[f, :, j].reshape(256, LANES)

    def arrived(f):
        return lambda j: recvs[f, :, j].reshape(256, LANES)

    for g in both:
        first = 0 if g == 0 else CHUNK[0]
        ky = waves[0, first : first + CHUNK[g], :] + waves[1, first : first + CHUNK[g], :] * me.astype(F32)

        def make_tables(c, g=g, ky=ky):
            rows = lax.broadcasted_iota(jnp.int32, (CHUNK[g], LANES), 0)
            lanes = lax.broadcasted_iota(jnp.int32, (CHUNK[g], LANES), 1)
            k = 4 * c + 16 * lanes
            for q in range(1, 4):
                k = k + jnp.where(rows >= q * ROWS_OF[g], 1, 0)
            kx = jnp.where(k < N // 2, k, k - N)
            kxf = kx.astype(F32)
            square = kxf * kxf + ky * ky
            decay = jnp.exp(-TIME_STEP * (DRAG + 9.0 * square / (N * N)))
            to = chunk(g, c)
            dx_t[to, :] = jnp.where(kx == -(N // 2), 0.0, kxf)
            linv_t[to, :] = jnp.where(square > 0.0, 1.0 / jnp.maximum(square, 1.0), 0.0)
            decay_t[to, :] = decay
            keep_mask = (3.0 * jnp.abs(kxf) <= N) & (3.0 * jnp.abs(ky) <= N)
            nlf_t[to, :] = jnp.where(keep_mask, TIME_STEP * decay, 0.0)

        loop(4, make_tables, 1)

    def zero_columns(b):
        recvs[5, b] = jnp.zeros((8, 2, 8, LANES), F32)

    @pl.when(me >= KEPT)
    def _():
        def clear(b):
            recvs[4, b] = jnp.zeros((8, 2, 8, LANES), F32)
            recvs[12, b] = jnp.zeros((8, 2, 8, LANES), F32)

        loop(16, clear, 1)

    loop(16 - KEPT, lambda b: zero_columns(b + KEPT), 1)
    flat[...] = jnp.zeros_like(flat)

    def two(re, im):
        return jnp.concatenate([re, im], axis=1)

    def halves(ref, rows):
        return ref[rows, 0:LANES], ref[rows, LANES : 2 * LANES]

    def psi_hat(rows):
        re, im = halves(w_spec, rows)
        linv = linv_t[rows, :]
        return two(linv * re, linv * im)

    def v_hat(rows):
        re, im = halves(w_spec, rows)
        factor = linv_t[rows, :] * dx_t[rows, :]
        return two(factor * im, -factor * re)

    def wx_hat(rows):
        re, im = halves(w_spec, rows)
        factor = dx_t[rows, :]
        return two(-factor * im, factor * re)

    def forward_columns(g, f, emit):
        col_forward(g, recvs.at[f], first_mask, col_mats, twiddle, col_s, emit)

    def inverse_columns(g, f, load):
        col_inverse(g, load, first_mask, col_mats, twiddle, col_s, sends.at[f])
        start(f, g)

    def put(ref):
        def emit(rows, c, value):
            ref[rows, :] = value
        return emit

    for g in both:
        finish(0, g)
        forward_columns(g, 0, put(w_spec))
        inverse_columns(g, 1, psi_hat)
        inverse_columns(g, 2, v_hat)
        inverse_columns(g, 3, wx_hat)
    start_side(10)

    table_copy(3).wait()
    for g in both:
        row_long_inverse(g, stacked(0), rowm.at[3], row_s.at[0])
    loop(16, lambda t: keep(grid_wy, t, row_short_inverse(t, row_s.at[0])))
    table_copy(2).wait()

    for g in both:
        finish(1, g)
        row_long_inverse(g, arrived(1), rowm.at[3], row_s.at[0])
        if g == 1:
            loop(16, lambda t: keep(grid_u, t, row_short_inverse(t, row_s.at[0])))
        finish(2, g)
        row_long_inverse(g, arrived(2), rowm.at[2], row_s.at[1])
        if g == 1:
            loop(16, lambda t: keep(grid_v, t, row_short_inverse(t, row_s.at[1])))
        finish(3, g)
        row_long_inverse(g, arrived(3), rowm.at[2], row_s.at[2])

    def nonlinear(t):
        tiles = row_short_inverse(t, row_s.at[2])
        product = []
        for b in range(16):
            grid_wx[b, tile(t), :] = tiles[b]
            product.append(
                grid_u[b, tile(t), :] * tiles[b] + grid_v[b, tile(t), :] * grid_wy[b, tile(t), :])
        row_short_forward(t, product, row_s.at[0])

    loop(16, nonlinear)
    for g in both:
        row_long_forward(g, rowm.at[0], row_s.at[0], sends.at[4])
        start(4, g)
    start_side(12)
    table_copy(1).wait()

    finish_side(10)
    for g in both:
        forward_columns(g, 10, put(next_start))

    def own_ky(g):
        rows = slice(0, CHUNK[0]) if g == 0 else slice(CHUNK[0], CHUNK[0] + CHUNK[1])
        return waves[0, rows, :] + waves[1, rows, :] * me.astype(F32)

    def end_of(g, rows, ref, value):
        re, im = halves(ref, rows)
        decay, nlf = decay_t[rows, :], nlf_t[rows, :]
        forced = (dx_t[rows, :] == 0.0) & (nlf > 0.0) & (own_ky(g) == float(FORCING_WAVE))
        force = jnp.where(forced, TIME_STEP * FORCE_AMP * (N * N / 2.0) * decay, 0.0)
        return (
            decay * re - nlf * value[:, 0:LANES] + force,
            decay * im - nlf * value[:, LANES : 2 * LANES],
        )

    def put_adjoint(g):
        def emit(rows, c, value):
            end_re, end_im = end_of(g, rows, w_spec, value)
            next_re, next_im = halves(next_start, rows)
            adj[rows, :] = two(end_re - next_re, end_im - next_im)
        return emit

    def weight_hat(rows):
        re, im = halves(adj, rows)
        nlf = nlf_t[rows, :]
        return two(nlf * re, nlf * im)

    for g in both:
        finish(4, g)
        forward_columns(g, 4, put_adjoint(g))
        inverse_columns(g, 5, weight_hat)
    start_side(11)

    for g in both:
        finish(5, g)
        row_long_inverse(g, arrived(5), rowm.at[2], row_s.at[0])

    def weighted(t):
        tiles = row_short_inverse(t, row_s.at[0])
        keep(grid_a, t, tiles)
        row_short_forward(t, [tiles[b] * grid_u[b, tile(t), :] for b in range(16)], row_s.at[1])

    def product(ref, scratch):
        def step(t):
            tiles = [grid_a[b, tile(t), :] * ref[b, tile(t), :] for b in range(16)]
            row_short_forward(t, tiles, scratch)
        return step

    loop(16, weighted)
    for g in both:
        row_long_forward(g, rowm.at[0], row_s.at[1], sends.at[6])
        start(6, g)
    for f, ref, mat in ((7, grid_wx, 1), (8, grid_wy, 0)):
        loop(16, product(ref, row_s.at[0]))
        for g in both:
            row_long_forward(g, rowm.at[mat], row_s.at[0], sends.at[f])
            start(f, g)
    loop(16, product(grid_v, row_s.at[0]))
    for g in both:
        row_long_forward(g, rowm.at[1], row_s.at[0], local_b)

    def put_residual(g):
        def emit(rows, c, value):
            prev_re, prev_im = end_of(g, rows, previous, value)
            re, im = halves(w_spec, rows)
            res_re, res_im = prev_re - re, prev_im - im
            residual[rows, :] = two(res_re, res_im)
            adj_re, adj_im = halves(adj, rows)
            decay = decay_t[rows, :]
            adj[rows, :] = two(decay * adj_re - res_re, decay * adj_im - res_im)
        return emit

    finish_side(11)
    for g in both:
        forward_columns(g, 11, put(previous))
    finish_side(12)
    for g in both:
        forward_columns(g, 12, put_residual(g))

    slots = slot_table()

    def write_residual(k, mirror, flip):
        for part in range(2):
            lanes = slice(part * LANES, (part + 1) * LANES)
            for j in range(8):
                direct = residual[tile_rows(k, j), lanes]
                mirrored = residual[tile_rows(mirror, j), lanes]
                if part:
                    mirrored = -mirrored
                for h in range(2):
                    to = int(slots[j, 4 * h])
                    flat[part, 0, pl.ds(to, 4, stride=16), :] = direct[4 * h : 4 * h + 4]
                    flat[part, 1, pl.ds(64 + to, 4, stride=16), :] = mirrored[4 * h : 4 * h + 4]
            extra = residual[tile_rows(k, 8), lanes]
            flat[part, 0, 64:72, :] = jnp.where(first_mask, extra, 0.0)
            flat[part, 1, 64:72, :] = jnp.where(first_mask, 0.0, flat[part, 1, 64:72, :])
            high, low = split(jnp.concatenate([flat[part, 0], flat[part, 1]], axis=1))
            contract = (((1,), (1,)), ((), ()))
            result = lax.dot_general(flip, high, contract, preferred_element_type=F32)
            result = result + lax.dot_general(flip, low, contract, preferred_element_type=F32)
            resid_v[part, :, k, :] = result

    write_residual(0, 0, flips[0])
    loop(15, lambda i: write_residual(i + 1, 15 - i, flips[1]), 1)
    resid_copy = pltpu.make_async_copy(resid_v, resid, out_sem.at[0])
    resid_copy.start()

    def add_a(rows, c, value):
        re, im = halves(adj, rows)
        dx = dx_t[rows, :]
        adj[rows, :] = two(re - dx * value[:, LANES : 2 * LANES], im + dx * value[:, 0:LANES])

    def add_c(rows, c, value):
        re, im = halves(adj, rows)
        linv = linv_t[rows, :]
        adj[rows, :] = two(re + linv * value[:, 0:LANES], im + linv * value[:, LANES : 2 * LANES])

    def add_d(rows, c, value):
        re, im = halves(adj, rows)
        factor = linv_t[rows, :] * dx_t[rows, :]
        adj[rows, :] = two(
            re + factor * value[:, LANES : 2 * LANES], im - factor * value[:, 0:LANES])

    for f, emit in ((6, add_a), (7, add_c), (8, add_d)):
        for g in both:
            finish(f, g)
            forward_columns(g, f, emit)
            if f == 8:
                inverse_columns(g, 9, lambda rows: adj[rows, :])

    def total(j):
        return (recvs[9, :, j] + local_b[:, j]).reshape(256, LANES)

    for g in both:
        finish(9, g)
        row_long_inverse(g, total, rowm.at[2], row_s.at[0])
    loop(16, lambda t: keep(grid_a, t, row_short_inverse(t, row_s.at[0])))
    for b in range(16):
        grad_v[:, b * LANES : (b + 1) * LANES] = grid_a[b].T
    grad_copy = pltpu.make_async_copy(grad_v, grad, out_sem.at[1])
    grad_copy.start()
    for f in range(10):
        for g in both:
            finish_send(f, g)
    wait_side(10, send_sem)
    wait_side(11, send_sem)
    wait_side(12, send_sem, KEPT)
    resid_copy.wait()
    grad_copy.wait()


def body(vorticity):
    col_mats, twiddle = col_tables()
    vmem = pl.BlockSpec(memory_space=pltpu.VMEM)
    hbm = pl.BlockSpec(memory_space=pl.ANY)
    slab = (16, 8, 2, 8, LANES)
    grid = pltpu.VMEM((16, LANES, LANES), F32)
    spectrum = pltpu.VMEM((ALL_ROWS, 2 * LANES), F32)
    factor = pltpu.VMEM((ALL_ROWS, LANES), F32)
    outs = ((LANES, N), (2, LANES, 16, LANES))
    gradient, residual = pl.pallas_call(
        kernel,
        out_shape=tuple(jax.ShapeDtypeStruct(shape, F32) for shape in outs),
        in_specs=[vmem, hbm, vmem, vmem, vmem, vmem],
        out_specs=(hbm, hbm),
        scratch_shapes=[
            pltpu.VMEM((4, 2, 8, 256, 256), BF16),
            grid, grid, grid, grid, grid,
            pltpu.VMEM((10,) + slab, F32),
            pltpu.VMEM((13,) + slab, F32),
            pltpu.VMEM(slab, F32),
            pltpu.VMEM((3, 8, 256, LANES), F32),
            spectrum, spectrum, spectrum, spectrum, spectrum, spectrum,
            factor, factor, factor, factor,
            pltpu.VMEM((2, 2, LANES, LANES), F32),
            pltpu.VMEM(outs[0], F32),
            pltpu.VMEM(outs[1], F32),
            pltpu.SemaphoreType.DMA((4,)),
            pltpu.SemaphoreType.DMA((2,)),
            pltpu.SemaphoreType.DMA((10, 2)),
            pltpu.SemaphoreType.DMA((13, 2)),
            pltpu.SemaphoreType.DMA((13, 2)),
        ],
        compiler_params=pltpu.CompilerParams(
            collective_id=0, has_side_effects=True, vmem_limit_bytes=62 * 2**20
        ),
        name="orbit_gradient",
    )(vorticity[0], jnp.asarray(row_tables()), jnp.asarray(col_mats), jnp.asarray(twiddle),
      jnp.asarray(flip_tables()), jnp.asarray(wave_table()))
    return gradient[None], residual.reshape(1, 2, N, LANES)


def solution(mesh):
    return jax.shard_map(
        body,
        mesh=mesh,
        in_specs=(P("seg", "space", None),),
        out_specs=(P("seg", "space", None), P("seg", None, None, "space")),
        check_vma=False,
    )
```

```python
import functools
import math

import jax
import jax.numpy as jnp
import ml_dtypes
import numpy as np
from jax import lax
from jax.experimental import pallas as pl
from jax.experimental.pallas import tpu as pltpu
from jax.sharding import PartitionSpec as P

N = 2048
SLABS = 16
LANES = 128
GROUPS = ((0, 8, 1, 2, 3), (4, 5, 6, 7))
GROUP_J = (0, 4)
ROWS_OF = (40, 32)
FIRST_ROW = (0, 640)
CHUNK = (160, 128)
ALL_ROWS = 16 * (40 + 32)
KEPT = 11
TIME_STEP = 0.3
DRAG = 0.05
FORCE_AMP = 0.8
FORCING_WAVE = 4
MESH = pl.DeviceIdType.MESH
F32 = jnp.float32
BF16 = jnp.bfloat16


def split_table(table):
    high = table.astype(np.float32).astype(ml_dtypes.bfloat16)
    low = (table - high.astype(np.float64)).astype(np.float32).astype(ml_dtypes.bfloat16)
    return high, low


def slot_wave(j, d, r):
    if r < 4:
        return j + 16 * (4 * d + r)
    return (16 - j if j else 8) + 16 * (4 * d + r - 4)


@functools.cache
def row_tables():
    a = np.arange(LANES)
    forward = np.zeros((8, 16, 2, 8, 2, LANES))
    inverse = np.zeros((8, 2, LANES, 16, 2, 8))
    wave = np.zeros((8, 16, 8))
    for j in range(8):
        for d in range(16):
            for r in range(8):
                k = slot_wave(j, d, r)
                wave[j, d, r] = k
                c = np.cos(2 * np.pi * ((a * k) % N) / N)
                s = np.sin(2 * np.pi * ((a * k) % N) / N)
                if j == 0:
                    part = 0 if r < 4 else 1
                    forward[j, d, 0, r, part] = c
                    forward[j, d, 1, r, part] = -s
                    inverse[j, part, :, d, 0, r] = 2 * c
                    inverse[j, part, :, d, 1, r] = -2 * s
                    if k == 0:
                        alternate = 1.0 - 2.0 * (a % 2)
                        forward[j, d, 1, r, part] = alternate
                        inverse[j, part, :, d, 0, r] = 1.0
                        inverse[j, part, :, d, 1, r] = alternate
                else:
                    sign = 1.0 if r < 4 else -1.0
                    forward[j, d, 0, r, 0] = c
                    forward[j, d, 0, r, 1] = sign * s
                    forward[j, d, 1, r, 0] = -s
                    forward[j, d, 1, r, 1] = sign * c
                    inverse[j, 0, :, d, 0, r] = c
                    inverse[j, 0, :, d, 1, r] = -s
                    inverse[j, 1, :, d, 0, r] = sign * s
                    inverse[j, 1, :, d, 1, r] = sign * c
    inverse /= N
    dwave = wave[:, :, None, :, None, None]
    forward_dy = np.stack([-forward[:, :, 1], forward[:, :, 0]], axis=2) * dwave
    inverse_dy = np.stack([inverse[..., 1, :], -inverse[..., 0, :]], axis=-2) * wave[:, None, None, :, None, :]
    shape = (8, 256, 256)
    outs = []
    for table in (forward, forward_dy, inverse, inverse_dy):
        high, low = split_table(table.reshape(shape))
        outs.append(np.stack([high, low]))
    return np.stack(outs)


@functools.cache
def col_tables():
    a = np.arange(LANES)
    angle = 2 * np.pi * (np.outer(a, a) % LANES) / LANES
    c, s = np.cos(angle), np.sin(angle)
    forward = np.block([[c, -s], [s, c]])
    inverse = np.block([[c, s], [-s, c]]) / N
    mats = np.stack([np.stack(split_table(m)) for m in (forward, inverse)])
    angle = 2 * np.pi * np.outer(np.arange(16), a) / N
    twiddle = np.stack([np.cos(angle), np.sin(angle)], axis=1)
    twiddle = np.broadcast_to(twiddle[:, :, None, :], (16, 2, 8, LANES)).astype(np.float32)
    return mats, np.ascontiguousarray(twiddle)


@functools.cache
def flip_tables():
    eye = np.eye(LANES)
    first = np.concatenate([eye, eye[(LANES - np.arange(LANES)) % LANES]], axis=1)
    other = np.concatenate([eye, eye[LANES - 1 - np.arange(LANES)]], axis=1)
    return (np.stack([first, other]) / N).astype(ml_dtypes.bfloat16)


@functools.cache
def slot_table():
    return np.array([[slot_wave(j, 0, r) for r in range(8)] for j in range(8)], np.int32)


@functools.cache
def wave_table():
    table = np.zeros((2, CHUNK[0] + CHUNK[1], LANES), np.float32)
    row = 0
    for group in GROUPS:
        for _ in range(4):
            for j in group:
                table[0, row : row + 8] = (N // 2) if j == 8 else slot_table()[j][:, None]
                table[1, row : row + 8] = 0 if j == 8 else 64
                row += 8
    return table


def times_root(re, im, k, n, sign):
    k = k % n
    if im is None:
        if k == 0:
            return re, None
        angle = sign * 2 * math.pi * k / n
        if 4 * k == n:
            return None, (re if sign > 0 else -re)
        return re * math.cos(angle), re * math.sin(angle)
    if k == 0:
        return re, im
    if 2 * k == n:
        return -re, -im
    if 4 * k == n:
        return (-im, re) if sign > 0 else (im, -re)
    if 4 * k == 3 * n:
        return (im, -re) if sign > 0 else (-im, re)
    angle = sign * 2 * math.pi * k / n
    c, s = math.cos(angle), math.sin(angle)
    if 8 * k == n or 8 * k == 3 * n or 8 * k == 5 * n or 8 * k == 7 * n:
        m = abs(c)
        rm, imm = re * m, im * m
        sc, ss = (1 if c > 0 else -1), (1 if s > 0 else -1)
        first = (rm if sc > 0 else -rm) - imm if ss > 0 else (rm if sc > 0 else -rm) + imm
        second = (imm if sc > 0 else -imm) + rm if ss > 0 else (imm if sc > 0 else -imm) - rm
        return first, second
    return re * c - im * s, re * s + im * c


def complex_fft(values, sign):
    n = len(values)
    if n == 1:
        return values
    even = complex_fft(values[0::2], sign)
    odd = complex_fft(values[1::2], sign)
    outs = [None] * n
    for k in range(n // 2):
        re, im = times_root(odd[k][0], odd[k][1], k, n, sign)
        outs[k] = (even[k][0] + re, even[k][1] + im)
        outs[k + n // 2] = (even[k][0] - re, even[k][1] - im)
    return outs


def real_fft(values):
    n = len(values)
    if n == 2:
        return [(values[0] + values[1], None), (values[0] - values[1], None)]
    even, odd = real_fft(values[0::2]), real_fft(values[1::2])
    half = n // 2
    outs = [None] * (half + 1)
    outs[0] = (even[0][0] + odd[0][0], None)
    outs[half] = (even[0][0] - odd[0][0], None)
    for k in range(1, half // 2 + 1):
        if 4 * k == n:
            outs[k] = (even[k][0], -odd[k][0])
            continue
        re, im = times_root(odd[k][0], odd[k][1], k, n, -1)
        outs[k] = (even[k][0] + re, even[k][1] + im)
        outs[half - k] = (even[k][0] - re, im - even[k][1])
    return outs


def real_inverse(values):
    half = len(values) - 1
    n = 2 * half
    if n == 2:
        return [values[0][0] + values[1][0], values[0][0] - values[1][0]]
    even, odd = [None] * (half // 2 + 1), [None] * (half // 2 + 1)
    even[0] = (values[0][0] + values[half][0], None)
    odd[0] = (values[0][0] - values[half][0], None)
    for k in range(1, half // 2 + 1):
        if 4 * k == n:
            even[k] = (values[k][0] * 2.0, None)
            odd[k] = (values[k][1] * -2.0, None)
            continue
        (ar, ai), (br, bi) = values[k], values[half - k]
        even[k] = (ar + br, ai - bi)
        odd[k] = times_root(ar - br, ai + bi, k, n, 1)
    low, high = real_inverse(even), real_inverse(odd)
    outs = [None] * n
    outs[0::2] = low
    outs[1::2] = high
    return outs


def split(values):
    high = values.astype(BF16)
    return high, (values - high.astype(F32)).astype(BF16)


def dot(a, b):
    return jnp.dot(a, b, preferred_element_type=F32)


def table_times(high, low, values):
    vh, vl = split(values)
    return dot(high, vh) + (dot(low, vh) + dot(high, vl))


def times_table(values, high, low):
    vh, vl = split(values)
    return dot(vh, high) + (dot(vh, low) + dot(vl, high))


def loop(count, step, unroll=4):
    lax.fori_loop(0, count, lambda i, c: (step(i), c)[1], 0, unroll=unroll)


def tile(t, base=0):
    return pl.ds(pl.multiple_of(base + t * 8, 8), 8)


def chunk(g, c):
    return pl.ds(pl.multiple_of(FIRST_ROW[g] + c * CHUNK[g], 8), CHUNK[g])


def tile_rows(k, j):
    g = 0 if j in GROUPS[0] else 1
    start = FIRST_ROW[g] + GROUPS[g].index(j) * 8
    if isinstance(k, int):
        return pl.ds(start + k * ROWS_OF[g], 8)
    return pl.ds(pl.multiple_of(start + k * ROWS_OF[g], 8), 8)


def row_short_forward(t, tiles, scratch):
    spectrum = real_fft(tiles)
    scratch[0, tile(t), :] = spectrum[0][0]
    scratch[0, tile(t, LANES), :] = spectrum[8][0]
    for j in range(1, 8):
        scratch[j, tile(t), :] = spectrum[j][0]
        scratch[j, tile(t, LANES), :] = spectrum[j][1]


def row_long_forward(g, mat, scratch, out):
    def step(i):
        j = i + GROUP_J[g]
        result = table_times(mat[0, j], mat[1, j], scratch[j])
        out[:, j] = result.reshape(16, 2, 8, LANES)

    loop(4, step)


def row_long_inverse(g, load, mat, scratch):
    def step(i):
        j = i + GROUP_J[g]
        scratch[j] = table_times(mat[0, j], mat[1, j], load(j))

    loop(4, step)


def row_short_inverse(t, scratch):
    spectrum = [(scratch[0, tile(t), :], None)]
    spectrum += [(scratch[j, tile(t), :], scratch[j, tile(t, LANES), :]) for j in range(1, 8)]
    spectrum.append((scratch[0, tile(t, LANES), :], None))
    return real_inverse(spectrum)


def col_forward(g, received, first_mask, mats, twiddle, scratch, emit):
    def transform(values, start):
        spectrum = complex_fft(values, -1)
        for k in range(16):
            re, im = spectrum[k]
            if k:
                c, s = twiddle[k, 0], twiddle[k, 1]
                re, im = re * c + im * s, im * c - re * s
            rows = pl.ds(start + k * ROWS_OF[g], 8)
            scratch[rows, 0:LANES] = re
            scratch[rows, LANES : 2 * LANES] = im

    for n, j in enumerate(GROUPS[g]):
        start = FIRST_ROW[g] + n * 8
        if j == 0:
            values = [
                (received[b, 0, 0], jnp.where(first_mask, 0.0, received[b, 0, 1])) for b in range(16)
            ]
        elif j == 8:
            zero = jnp.zeros((8, LANES), F32)
            values = [(jnp.where(first_mask, received[b, 0, 1], 0.0), zero) for b in range(16)]
        else:
            values = [(received[b, j, 0], received[b, j, 1]) for b in range(16)]
        transform(values, start)

    def step(c):
        rows = chunk(g, c)
        emit(rows, c, times_table(scratch[rows, :], mats[0, 0], mats[0, 1]))

    loop(4, step)


def col_inverse(g, load, first_mask, mats, twiddle, scratch, out):
    def step(c):
        rows = chunk(g, c)
        scratch[rows, :] = times_table(load(rows), mats[1, 0], mats[1, 1])

    loop(4, step)

    def transform(n):
        values = []
        for k in range(16):
            rows = pl.ds(FIRST_ROW[g] + n * 8 + k * ROWS_OF[g], 8)
            re = scratch[rows, 0:LANES]
            im = scratch[rows, LANES : 2 * LANES]
            if k:
                c, s = twiddle[k, 0], twiddle[k, 1]
                re, im = re * c - im * s, im * c + re * s
            values.append((re, im))
        return complex_fft(values, 1)

    if g == 0:
        for b, (re, im) in enumerate(transform(1)):
            out[b, 0, 0] = re
        for b, (re, im) in enumerate(transform(0)):
            out[b, 0, 1] = jnp.where(first_mask, out[b, 0, 0], im)
            out[b, 0, 0] = re
    for n, j in enumerate(GROUPS[g]):
        if j not in (0, 8):
            for b, (re, im) in enumerate(transform(n)):
                out[b, j, 0] = re
                out[b, j, 1] = im


def partners(me):
    core = me % 2
    step = [(1 - 2 * ((me // (1 << k)) % 2)) * (1 << k) for k in range(4)]

    def other(offset):
        return me + sum(step[k] for k in range(4) if (offset >> k) & 1)

    return [other(i) * (1 - core) + other(16 - i) * core for i in range(1, 16)]


def kernel(
    vort, row_hbm, col_mats, twiddle, flips, waves,
    grad, resid,
    rowm, grid_a, grid_u, grid_v, grid_wx, grid_wy, sends, recvs, local_b,
    row_s, col_s, w_spec, previous, adj, next_start, residual,
    dx_t, linv_t, decay_t, nlf_t, flat, grad_v, resid_v,
    table_sem, out_sem, own_sem, send_sem, recv_sem,
):
    me = lax.axis_index("space")
    seg = lax.axis_index("seg")
    after, before = (seg + 1) % 8, (seg + 7) % 8
    rows_in_tile = lax.broadcasted_iota(jnp.int32, (8, LANES), 0)
    first_mask = (rows_in_tile == 0) & (jnp.zeros((8, LANES), jnp.int32) + me == 0)
    others = partners(me)
    both = (0, 1)

    def table_copy(i):
        return pltpu.make_async_copy(row_hbm.at[i], rowm.at[i], table_sem.at[i])

    for i in (0, 3, 2, 1):
        table_copy(i).start()

    barrier = pltpu.get_barrier_semaphore()
    for p in others:
        pl.semaphore_signal(barrier, inc=1, device_id={"space": p}, device_id_type=MESH)
    for s in (after, before):
        for p in others + [me]:
            pl.semaphore_signal(
                barrier, inc=1, device_id={"seg": s, "space": p}, device_id_type=MESH)

    def part(f, g, p):
        return (f, p, pl.ds(GROUP_J[g], 4))

    def own_copy(f, g):
        return pltpu.make_async_copy(
            sends.at[part(f, g, me)], recvs.at[part(f, g, me)], own_sem.at[f, g])

    def start(f, g):
        own_copy(f, g).start()

        def one(p):
            pltpu.make_async_remote_copy(
                src_ref=sends.at[part(f, g, p)], dst_ref=recvs.at[part(f, g, me)],
                send_sem=send_sem.at[f, g], recv_sem=recv_sem.at[f, g],
                device_id={"space": p}, device_id_type=MESH).start()

        if f == 4:
            for p in others:
                pl.when(p < KEPT)(functools.partial(one, p))
        elif f == 5:
            @pl.when(me < KEPT)
            def _():
                for p in others:
                    one(p)
        else:
            for p in others:
                one(p)

    def wait_bytes(f, g, sem, count):
        pltpu.make_async_copy(
            sends.at[part(f, g, pl.ds(0, count))], recvs.at[part(f, g, pl.ds(0, count))],
            sem.at[f, g]).wait()

    def some(f, g, sem):
        @pl.when(me < KEPT)
        def _():
            wait_bytes(f, g, sem, KEPT - 1)

        @pl.when(me >= KEPT)
        def _():
            wait_bytes(f, g, sem, KEPT)

    def inside(f, g, sem):
        @pl.when(me < KEPT)
        def _():
            wait_bytes(f, g, sem, 15)

    def finish(f, g):
        own_copy(f, g).wait()
        kind = {4: inside, 5: some}.get(f)
        if kind:
            kind(f, g, recv_sem)
        else:
            wait_bytes(f, g, recv_sem, 15)

    def finish_send(f, g):
        kind = {4: some, 5: inside}.get(f)
        if kind:
            kind(f, g, send_sem)
        else:
            wait_bytes(f, g, send_sem, 15)

    side = {10: (0, before), 11: (0, after), 12: (4, after)}

    def start_side(f):
        source, s = side[f]

        def one(p):
            pltpu.make_async_remote_copy(
                src_ref=sends.at[source, p], dst_ref=recvs.at[f, me],
                send_sem=send_sem.at[f, 0], recv_sem=recv_sem.at[f, 0],
                device_id={"seg": s, "space": p}, device_id_type=MESH).start()

        for p in [me] + others:
            if f == 12:
                pl.when(p < KEPT)(functools.partial(one, p))
            else:
                one(p)

    def wait_side(f, sem, count=16):
        pltpu.make_async_copy(
            sends.at[side[f][0], pl.ds(0, count)], recvs.at[f, pl.ds(0, count)], sem.at[f, 0]).wait()

    def finish_side(f):
        if f == 12:
            pl.when(me < KEPT)(lambda: wait_side(f, recv_sem))
        else:
            wait_side(f, recv_sem)

    for b in range(16):
        grid_a[b] = vort[:, b * LANES : (b + 1) * LANES].T

    def tiles_of(ref, t):
        return [ref[b, tile(t), :] for b in range(16)]

    def keep(ref, t, tiles):
        for b in range(16):
            ref[b, tile(t), :] = tiles[b]

    loop(16, lambda t: row_short_forward(t, tiles_of(grid_a, t), row_s.at[0]))
    table_copy(0).wait()
    for g in both:
        row_long_forward(g, rowm.at[0], row_s.at[0], sends.at[0])
        if g == 0:
            pl.semaphore_wait(barrier, 47)
        start(0, g)

    def stacked(f):
        return lambda j: sends[f, :, j].reshape(256, LANES)

    def arrived(f):
        return lambda j: recvs[f, :, j].reshape(256, LANES)

    for g in both:
        first = 0 if g == 0 else CHUNK[0]
        ky = waves[0, first : first + CHUNK[g], :] + waves[1, first : first + CHUNK[g], :] * me.astype(F32)

        def make_tables(c, g=g, ky=ky):
            rows = lax.broadcasted_iota(jnp.int32, (CHUNK[g], LANES), 0)
            lanes = lax.broadcasted_iota(jnp.int32, (CHUNK[g], LANES), 1)
            k = 4 * c + 16 * lanes
            for q in range(1, 4):
                k = k + jnp.where(rows >= q * ROWS_OF[g], 1, 0)
            kx = jnp.where(k < N // 2, k, k - N)
            kxf = kx.astype(F32)
            square = kxf * kxf + ky * ky
            decay = jnp.exp(-TIME_STEP * (DRAG + 9.0 * square / (N * N)))
            to = chunk(g, c)
            dx_t[to, :] = jnp.where(kx == -(N // 2), 0.0, kxf)
            linv_t[to, :] = jnp.where(square > 0.0, 1.0 / jnp.maximum(square, 1.0), 0.0)
            decay_t[to, :] = decay
            keep_mask = (3.0 * jnp.abs(kxf) <= N) & (3.0 * jnp.abs(ky) <= N)
            nlf_t[to, :] = jnp.where(keep_mask, TIME_STEP * decay, 0.0)

        loop(4, make_tables, 1)

    def zero_columns(b):
        recvs[5, b] = jnp.zeros((8, 2, 8, LANES), F32)

    @pl.when(me >= KEPT)
    def _():
        def clear(b):
            recvs[4, b] = jnp.zeros((8, 2, 8, LANES), F32)
            recvs[12, b] = jnp.zeros((8, 2, 8, LANES), F32)

        loop(16, clear, 1)

    loop(16 - KEPT, lambda b: zero_columns(b + KEPT), 1)
    flat[...] = jnp.zeros_like(flat)

    def two(re, im):
        return jnp.concatenate([re, im], axis=1)

    def halves(ref, rows):
        return ref[rows, 0:LANES], ref[rows, LANES : 2 * LANES]

    def psi_hat(rows):
        re, im = halves(w_spec, rows)
        linv = linv_t[rows, :]
        return two(linv * re, linv * im)

    def v_hat(rows):
        re, im = halves(w_spec, rows)
        factor = linv_t[rows, :] * dx_t[rows, :]
        return two(factor * im, -factor * re)

    def wx_hat(rows):
        re, im = halves(w_spec, rows)
        factor = dx_t[rows, :]
        return two(-factor * im, factor * re)

    def forward_columns(g, f, emit):
        col_forward(g, recvs.at[f], first_mask, col_mats, twiddle, col_s, emit)

    def inverse_columns(g, f, load):
        col_inverse(g, load, first_mask, col_mats, twiddle, col_s, sends.at[f])
        start(f, g)

    def put(ref):
        def emit(rows, c, value):
            ref[rows, :] = value
        return emit

    for g in both:
        finish(0, g)
        forward_columns(g, 0, put(w_spec))
        inverse_columns(g, 1, psi_hat)
        inverse_columns(g, 2, v_hat)
        inverse_columns(g, 3, wx_hat)

    table_copy(3).wait()
    for g in both:
        row_long_inverse(g, stacked(0), rowm.at[3], row_s.at[0])
    loop(16, lambda t: keep(grid_wy, t, row_short_inverse(t, row_s.at[0])))
    table_copy(2).wait()

    for g in both:
        finish(1, g)
        row_long_inverse(g, arrived(1), rowm.at[3], row_s.at[0])
        if g == 1:
            loop(16, lambda t: keep(grid_u, t, row_short_inverse(t, row_s.at[0])))
        finish(2, g)
        row_long_inverse(g, arrived(2), rowm.at[2], row_s.at[1])
        if g == 1:
            loop(16, lambda t: keep(grid_v, t, row_short_inverse(t, row_s.at[1])))
        if g == 1:
            finish_send(3, 1)
            start_side(10)
        finish(3, g)
        row_long_inverse(g, arrived(3), rowm.at[2], row_s.at[2])

    def nonlinear(t):
        tiles = row_short_inverse(t, row_s.at[2])
        product = []
        for b in range(16):
            grid_wx[b, tile(t), :] = tiles[b]
            product.append(
                grid_u[b, tile(t), :] * tiles[b] + grid_v[b, tile(t), :] * grid_wy[b, tile(t), :])
        row_short_forward(t, product, row_s.at[0])

    loop(16, nonlinear)
    for g in both:
        row_long_forward(g, rowm.at[0], row_s.at[0], sends.at[4])
        start(4, g)
    start_side(12)
    table_copy(1).wait()

    finish_side(10)
    for g in both:
        forward_columns(g, 10, put(next_start))

    def own_ky(g):
        rows = slice(0, CHUNK[0]) if g == 0 else slice(CHUNK[0], CHUNK[0] + CHUNK[1])
        return waves[0, rows, :] + waves[1, rows, :] * me.astype(F32)

    def end_of(g, rows, ref, value):
        re, im = halves(ref, rows)
        decay, nlf = decay_t[rows, :], nlf_t[rows, :]
        forced = (dx_t[rows, :] == 0.0) & (nlf > 0.0) & (own_ky(g) == float(FORCING_WAVE))
        force = jnp.where(forced, TIME_STEP * FORCE_AMP * (N * N / 2.0) * decay, 0.0)
        return (
            decay * re - nlf * value[:, 0:LANES] + force,
            decay * im - nlf * value[:, LANES : 2 * LANES],
        )

    def put_adjoint(g):
        def emit(rows, c, value):
            end_re, end_im = end_of(g, rows, w_spec, value)
            next_re, next_im = halves(next_start, rows)
            adj[rows, :] = two(end_re - next_re, end_im - next_im)
        return emit

    def weight_hat(rows):
        re, im = halves(adj, rows)
        nlf = nlf_t[rows, :]
        return two(nlf * re, nlf * im)

    for g in both:
        finish(4, g)
        forward_columns(g, 4, put_adjoint(g))
        inverse_columns(g, 5, weight_hat)
    start_side(11)

    for g in both:
        finish(5, g)
        row_long_inverse(g, arrived(5), rowm.at[2], row_s.at[0])

    def weighted(t):
        tiles = row_short_inverse(t, row_s.at[0])
        keep(grid_a, t, tiles)
        row_short_forward(t, [tiles[b] * grid_u[b, tile(t), :] for b in range(16)], row_s.at[1])

    def product(ref, scratch):
        def step(t):
            tiles = [grid_a[b, tile(t), :] * ref[b, tile(t), :] for b in range(16)]
            row_short_forward(t, tiles, scratch)
        return step

    loop(16, weighted)
    for g in both:
        row_long_forward(g, rowm.at[0], row_s.at[1], sends.at[6])
        start(6, g)
    for f, ref, mat in ((7, grid_wx, 1), (8, grid_wy, 0)):
        loop(16, product(ref, row_s.at[0]))
        for g in both:
            row_long_forward(g, rowm.at[mat], row_s.at[0], sends.at[f])
            start(f, g)
    loop(16, product(grid_v, row_s.at[0]))
    for g in both:
        row_long_forward(g, rowm.at[1], row_s.at[0], local_b)

    def put_residual(g):
        def emit(rows, c, value):
            prev_re, prev_im = end_of(g, rows, previous, value)
            re, im = halves(w_spec, rows)
            res_re, res_im = prev_re - re, prev_im - im
            residual[rows, :] = two(res_re, res_im)
            adj_re, adj_im = halves(adj, rows)
            decay = decay_t[rows, :]
            adj[rows, :] = two(decay * adj_re - res_re, decay * adj_im - res_im)
        return emit

    finish_side(11)
    for g in both:
        forward_columns(g, 11, put(previous))
    finish_side(12)
    for g in both:
        forward_columns(g, 12, put_residual(g))

    slots = slot_table()

    def write_residual(k, mirror, flip):
        for part in range(2):
            lanes = slice(part * LANES, (part + 1) * LANES)
            for j in range(8):
                direct = residual[tile_rows(k, j), lanes]
                mirrored = residual[tile_rows(mirror, j), lanes]
                if part:
                    mirrored = -mirrored
                for h in range(2):
                    to = int(slots[j, 4 * h])
                    flat[part, 0, pl.ds(to, 4, stride=16), :] = direct[4 * h : 4 * h + 4]
                    flat[part, 1, pl.ds(64 + to, 4, stride=16), :] = mirrored[4 * h : 4 * h + 4]
            extra = residual[tile_rows(k, 8), lanes]
            flat[part, 0, 64:72, :] = jnp.where(first_mask, extra, 0.0)
            flat[part, 1, 64:72, :] = jnp.where(first_mask, 0.0, flat[part, 1, 64:72, :])
            high, low = split(jnp.concatenate([flat[part, 0], flat[part, 1]], axis=1))
            contract = (((1,), (1,)), ((), ()))
            result = lax.dot_general(flip, high, contract, preferred_element_type=F32)
            result = result + lax.dot_general(flip, low, contract, preferred_element_type=F32)
            resid_v[part, :, k, :] = result

    write_residual(0, 0, flips[0])
    loop(15, lambda i: write_residual(i + 1, 15 - i, flips[1]), 1)
    resid_copy = pltpu.make_async_copy(resid_v, resid, out_sem.at[0])
    resid_copy.start()

    def add_a(rows, c, value):
        re, im = halves(adj, rows)
        dx = dx_t[rows, :]
        adj[rows, :] = two(re - dx * value[:, LANES : 2 * LANES], im + dx * value[:, 0:LANES])

    def add_c(rows, c, value):
        re, im = halves(adj, rows)
        linv = linv_t[rows, :]
        adj[rows, :] = two(re + linv * value[:, 0:LANES], im + linv * value[:, LANES : 2 * LANES])

    def add_d(rows, c, value):
        re, im = halves(adj, rows)
        factor = linv_t[rows, :] * dx_t[rows, :]
        adj[rows, :] = two(
            re + factor * value[:, LANES : 2 * LANES], im - factor * value[:, 0:LANES])

    for f, emit in ((6, add_a), (7, add_c), (8, add_d)):
        for g in both:
            finish(f, g)
            forward_columns(g, f, emit)
            if f == 8:
                inverse_columns(g, 9, lambda rows: adj[rows, :])

    def total(j):
        return (recvs[9, :, j] + local_b[:, j]).reshape(256, LANES)

    for g in both:
        finish(9, g)
        row_long_inverse(g, total, rowm.at[2], row_s.at[0])
    loop(16, lambda t: keep(grid_a, t, row_short_inverse(t, row_s.at[0])))
    for b in range(16):
        grad_v[:, b * LANES : (b + 1) * LANES] = grid_a[b].T
    grad_copy = pltpu.make_async_copy(grad_v, grad, out_sem.at[1])
    grad_copy.start()
    for f in range(10):
        for g in both:
            if (f, g) != (3, 1):
                finish_send(f, g)
    wait_side(10, send_sem)
    wait_side(11, send_sem)
    wait_side(12, send_sem, KEPT)
    resid_copy.wait()
    grad_copy.wait()


def body(vorticity):
    col_mats, twiddle = col_tables()
    vmem = pl.BlockSpec(memory_space=pltpu.VMEM)
    hbm = pl.BlockSpec(memory_space=pl.ANY)
    slab = (16, 8, 2, 8, LANES)
    grid = pltpu.VMEM((16, LANES, LANES), F32)
    spectrum = pltpu.VMEM((ALL_ROWS, 2 * LANES), F32)
    factor = pltpu.VMEM((ALL_ROWS, LANES), F32)
    outs = ((LANES, N), (2, LANES, 16, LANES))
    gradient, residual = pl.pallas_call(
        kernel,
        out_shape=tuple(jax.ShapeDtypeStruct(shape, F32) for shape in outs),
        in_specs=[vmem, hbm, vmem, vmem, vmem, vmem],
        out_specs=(hbm, hbm),
        scratch_shapes=[
            pltpu.VMEM((4, 2, 8, 256, 256), BF16),
            grid, grid, grid, grid, grid,
            pltpu.VMEM((10,) + slab, F32),
            pltpu.VMEM((13,) + slab, F32),
            pltpu.VMEM(slab, F32),
            pltpu.VMEM((3, 8, 256, LANES), F32),
            spectrum, spectrum, spectrum, spectrum, spectrum, spectrum,
            factor, factor, factor, factor,
            pltpu.VMEM((2, 2, LANES, LANES), F32),
            pltpu.VMEM(outs[0], F32),
            pltpu.VMEM(outs[1], F32),
            pltpu.SemaphoreType.DMA((4,)),
            pltpu.SemaphoreType.DMA((2,)),
            pltpu.SemaphoreType.DMA((10, 2)),
            pltpu.SemaphoreType.DMA((13, 2)),
            pltpu.SemaphoreType.DMA((13, 2)),
        ],
        compiler_params=pltpu.CompilerParams(
            collective_id=0, has_side_effects=True, vmem_limit_bytes=62 * 2**20
        ),
        name="orbit_gradient",
    )(vorticity[0], jnp.asarray(row_tables()), jnp.asarray(col_mats), jnp.asarray(twiddle),
      jnp.asarray(flip_tables()), jnp.asarray(wave_table()))
    return gradient[None], residual.reshape(1, 2, N, LANES)


def solution(mesh):
    return jax.shard_map(
        body,
        mesh=mesh,
        in_specs=(P("seg", "space", None),),
        out_specs=(P("seg", "space", None), P("seg", None, None, "space")),
        check_vma=False,
    )
```

```python
import functools
import math

import jax
import jax.numpy as jnp
import ml_dtypes
import numpy as np
from jax import lax
from jax.experimental import pallas as pl
from jax.experimental.pallas import tpu as pltpu
from jax.sharding import PartitionSpec as P

N = 2048
SLABS = 16
LANES = 128
GROUPS = ((0, 8, 1, 2, 3), (4, 5, 6, 7))
GROUP_J = (0, 4)
ROWS_OF = (40, 32)
FIRST_ROW = (0, 640)
CHUNK = (160, 128)
ALL_ROWS = 16 * (40 + 32)
KEPT = 11
TIME_STEP = 0.3
DRAG = 0.05
FORCE_AMP = 0.8
FORCING_WAVE = 4
MESH = pl.DeviceIdType.MESH
F32 = jnp.float32
BF16 = jnp.bfloat16


def split_table(table):
    high = table.astype(np.float32).astype(ml_dtypes.bfloat16)
    low = (table - high.astype(np.float64)).astype(np.float32).astype(ml_dtypes.bfloat16)
    return high, low


def slot_wave(j, d, r):
    if r < 4:
        return j + 16 * (4 * d + r)
    return (16 - j if j else 8) + 16 * (4 * d + r - 4)


@functools.cache
def row_tables():
    a = np.arange(LANES)
    forward = np.zeros((8, 16, 2, 8, 2, LANES))
    inverse = np.zeros((8, 2, LANES, 16, 2, 8))
    wave = np.zeros((8, 16, 8))
    for j in range(8):
        for d in range(16):
            for r in range(8):
                k = slot_wave(j, d, r)
                wave[j, d, r] = k
                c = np.cos(2 * np.pi * ((a * k) % N) / N)
                s = np.sin(2 * np.pi * ((a * k) % N) / N)
                if j == 0:
                    part = 0 if r < 4 else 1
                    forward[j, d, 0, r, part] = c
                    forward[j, d, 1, r, part] = -s
                    inverse[j, part, :, d, 0, r] = 2 * c
                    inverse[j, part, :, d, 1, r] = -2 * s
                    if k == 0:
                        alternate = 1.0 - 2.0 * (a % 2)
                        forward[j, d, 1, r, part] = alternate
                        inverse[j, part, :, d, 0, r] = 1.0
                        inverse[j, part, :, d, 1, r] = alternate
                else:
                    sign = 1.0 if r < 4 else -1.0
                    forward[j, d, 0, r, 0] = c
                    forward[j, d, 0, r, 1] = sign * s
                    forward[j, d, 1, r, 0] = -s
                    forward[j, d, 1, r, 1] = sign * c
                    inverse[j, 0, :, d, 0, r] = c
                    inverse[j, 0, :, d, 1, r] = -s
                    inverse[j, 1, :, d, 0, r] = sign * s
                    inverse[j, 1, :, d, 1, r] = sign * c
    inverse /= N
    dwave = wave[:, :, None, :, None, None]
    forward_dy = np.stack([-forward[:, :, 1], forward[:, :, 0]], axis=2) * dwave
    inverse_dy = np.stack([inverse[..., 1, :], -inverse[..., 0, :]], axis=-2) * wave[:, None, None, :, None, :]
    shape = (8, 256, 256)
    outs = []
    for table in (forward, forward_dy, inverse, inverse_dy):
        high, low = split_table(table.reshape(shape))
        outs.append(np.stack([high, low]))
    return np.stack(outs)


@functools.cache
def col_tables():
    a = np.arange(LANES)
    angle = 2 * np.pi * (np.outer(a, a) % LANES) / LANES
    c, s = np.cos(angle), np.sin(angle)
    forward = np.block([[c, -s], [s, c]])
    inverse = np.block([[c, s], [-s, c]]) / N
    mats = np.stack([np.stack(split_table(m)) for m in (forward, inverse)])
    angle = 2 * np.pi * np.outer(np.arange(16), a) / N
    twiddle = np.stack([np.cos(angle), np.sin(angle)], axis=1)
    twiddle = np.broadcast_to(twiddle[:, :, None, :], (16, 2, 8, LANES)).astype(np.float32)
    return mats, np.ascontiguousarray(twiddle)


@functools.cache
def flip_tables():
    eye = np.eye(LANES)
    first = np.concatenate([eye, eye[(LANES - np.arange(LANES)) % LANES]], axis=1)
    other = np.concatenate([eye, eye[LANES - 1 - np.arange(LANES)]], axis=1)
    return (np.stack([first, other]) / N).astype(ml_dtypes.bfloat16)


@functools.cache
def slot_table():
    return np.array([[slot_wave(j, 0, r) for r in range(8)] for j in range(8)], np.int32)


@functools.cache
def wave_table():
    table = np.zeros((2, CHUNK[0] + CHUNK[1], LANES), np.float32)
    row = 0
    for group in GROUPS:
        for _ in range(4):
            for j in group:
                table[0, row : row + 8] = (N // 2) if j == 8 else slot_table()[j][:, None]
                table[1, row : row + 8] = 0 if j == 8 else 64
                row += 8
    return table


def times_root(re, im, k, n, sign):
    k = k % n
    if im is None:
        if k == 0:
            return re, None
        angle = sign * 2 * math.pi * k / n
        if 4 * k == n:
            return None, (re if sign > 0 else -re)
        return re * math.cos(angle), re * math.sin(angle)
    if k == 0:
        return re, im
    if 2 * k == n:
        return -re, -im
    if 4 * k == n:
        return (-im, re) if sign > 0 else (im, -re)
    if 4 * k == 3 * n:
        return (im, -re) if sign > 0 else (-im, re)
    angle = sign * 2 * math.pi * k / n
    c, s = math.cos(angle), math.sin(angle)
    if 8 * k == n or 8 * k == 3 * n or 8 * k == 5 * n or 8 * k == 7 * n:
        m = abs(c)
        rm, imm = re * m, im * m
        sc, ss = (1 if c > 0 else -1), (1 if s > 0 else -1)
        first = (rm if sc > 0 else -rm) - imm if ss > 0 else (rm if sc > 0 else -rm) + imm
        second = (imm if sc > 0 else -imm) + rm if ss > 0 else (imm if sc > 0 else -imm) - rm
        return first, second
    return re * c - im * s, re * s + im * c


def complex_fft(values, sign):
    n = len(values)
    if n == 1:
        return values
    even = complex_fft(values[0::2], sign)
    odd = complex_fft(values[1::2], sign)
    outs = [None] * n
    for k in range(n // 2):
        re, im = times_root(odd[k][0], odd[k][1], k, n, sign)
        outs[k] = (even[k][0] + re, even[k][1] + im)
        outs[k + n // 2] = (even[k][0] - re, even[k][1] - im)
    return outs


def real_fft(values):
    n = len(values)
    if n == 2:
        return [(values[0] + values[1], None), (values[0] - values[1], None)]
    even, odd = real_fft(values[0::2]), real_fft(values[1::2])
    half = n // 2
    outs = [None] * (half + 1)
    outs[0] = (even[0][0] + odd[0][0], None)
    outs[half] = (even[0][0] - odd[0][0], None)
    for k in range(1, half // 2 + 1):
        if 4 * k == n:
            outs[k] = (even[k][0], -odd[k][0])
            continue
        re, im = times_root(odd[k][0], odd[k][1], k, n, -1)
        outs[k] = (even[k][0] + re, even[k][1] + im)
        outs[half - k] = (even[k][0] - re, im - even[k][1])
    return outs


def real_inverse(values):
    half = len(values) - 1
    n = 2 * half
    if n == 2:
        return [values[0][0] + values[1][0], values[0][0] - values[1][0]]
    even, odd = [None] * (half // 2 + 1), [None] * (half // 2 + 1)
    even[0] = (values[0][0] + values[half][0], None)
    odd[0] = (values[0][0] - values[half][0], None)
    for k in range(1, half // 2 + 1):
        if 4 * k == n:
            even[k] = (values[k][0] * 2.0, None)
            odd[k] = (values[k][1] * -2.0, None)
            continue
        (ar, ai), (br, bi) = values[k], values[half - k]
        even[k] = (ar + br, ai - bi)
        odd[k] = times_root(ar - br, ai + bi, k, n, 1)
    low, high = real_inverse(even), real_inverse(odd)
    outs = [None] * n
    outs[0::2] = low
    outs[1::2] = high
    return outs


def split(values):
    high = values.astype(BF16)
    return high, (values - high.astype(F32)).astype(BF16)


def dot(a, b):
    return jnp.dot(a, b, preferred_element_type=F32)


def table_times(high, low, values):
    vh, vl = split(values)
    return dot(high, vh) + (dot(low, vh) + dot(high, vl))


def times_table(values, high, low):
    vh, vl = split(values)
    return dot(vh, high) + (dot(vh, low) + dot(vl, high))


def loop(count, step, unroll=4):
    lax.fori_loop(0, count, lambda i, c: (step(i), c)[1], 0, unroll=unroll)


def tile(t, base=0):
    return pl.ds(pl.multiple_of(base + t * 8, 8), 8)


def chunk(g, c):
    return pl.ds(pl.multiple_of(FIRST_ROW[g] + c * CHUNK[g], 8), CHUNK[g])


def tile_rows(k, j):
    g = 0 if j in GROUPS[0] else 1
    start = FIRST_ROW[g] + GROUPS[g].index(j) * 8
    if isinstance(k, int):
        return pl.ds(start + k * ROWS_OF[g], 8)
    return pl.ds(pl.multiple_of(start + k * ROWS_OF[g], 8), 8)


def row_short_forward(t, tiles, scratch):
    spectrum = real_fft(tiles)
    scratch[0, tile(t), :] = spectrum[0][0]
    scratch[0, tile(t, LANES), :] = spectrum[8][0]
    for j in range(1, 8):
        scratch[j, tile(t), :] = spectrum[j][0]
        scratch[j, tile(t, LANES), :] = spectrum[j][1]


def row_long_forward(g, mat, scratch, out):
    def step(i):
        j = i + GROUP_J[g]
        result = table_times(mat[0, j], mat[1, j], scratch[j])
        out[:, j] = result.reshape(16, 2, 8, LANES)

    loop(4, step)


def row_long_inverse(g, load, mat, scratch):
    def step(i):
        j = i + GROUP_J[g]
        scratch[j] = table_times(mat[0, j], mat[1, j], load(j))

    loop(4, step)


def row_short_inverse(t, scratch):
    spectrum = [(scratch[0, tile(t), :], None)]
    spectrum += [(scratch[j, tile(t), :], scratch[j, tile(t, LANES), :]) for j in range(1, 8)]
    spectrum.append((scratch[0, tile(t, LANES), :], None))
    return real_inverse(spectrum)


def col_forward(g, received, first_mask, mats, twiddle, scratch, emit):
    def transform(values, start):
        spectrum = complex_fft(values, -1)
        for k in range(16):
            re, im = spectrum[k]
            if k:
                c, s = twiddle[k, 0], twiddle[k, 1]
                re, im = re * c + im * s, im * c - re * s
            rows = pl.ds(start + k * ROWS_OF[g], 8)
            scratch[rows, 0:LANES] = re
            scratch[rows, LANES : 2 * LANES] = im

    for n, j in enumerate(GROUPS[g]):
        start = FIRST_ROW[g] + n * 8
        if j == 0:
            values = [
                (received[b, 0, 0], jnp.where(first_mask, 0.0, received[b, 0, 1])) for b in range(16)
            ]
        elif j == 8:
            zero = jnp.zeros((8, LANES), F32)
            values = [(jnp.where(first_mask, received[b, 0, 1], 0.0), zero) for b in range(16)]
        else:
            values = [(received[b, j, 0], received[b, j, 1]) for b in range(16)]
        transform(values, start)

    def step(c):
        rows = chunk(g, c)
        emit(rows, c, times_table(scratch[rows, :], mats[0, 0], mats[0, 1]))

    loop(4, step)


def col_inverse(g, load, first_mask, mats, twiddle, scratch, out):
    def step(c):
        rows = chunk(g, c)
        scratch[rows, :] = times_table(load(rows), mats[1, 0], mats[1, 1])

    loop(4, step)

    def transform(n):
        values = []
        for k in range(16):
            rows = pl.ds(FIRST_ROW[g] + n * 8 + k * ROWS_OF[g], 8)
            re = scratch[rows, 0:LANES]
            im = scratch[rows, LANES : 2 * LANES]
            if k:
                c, s = twiddle[k, 0], twiddle[k, 1]
                re, im = re * c - im * s, im * c + re * s
            values.append((re, im))
        return complex_fft(values, 1)

    if g == 0:
        for b, (re, im) in enumerate(transform(1)):
            out[b, 0, 0] = re
        for b, (re, im) in enumerate(transform(0)):
            out[b, 0, 1] = jnp.where(first_mask, out[b, 0, 0], im)
            out[b, 0, 0] = re
    for n, j in enumerate(GROUPS[g]):
        if j not in (0, 8):
            for b, (re, im) in enumerate(transform(n)):
                out[b, j, 0] = re
                out[b, j, 1] = im


def partners(me):
    core = me % 2
    step = [(1 - 2 * ((me // (1 << k)) % 2)) * (1 << k) for k in range(4)]

    def other(offset):
        return me + sum(step[k] for k in range(4) if (offset >> k) & 1)

    return [other(i) * (1 - core) + other(16 - i) * core for i in range(1, 16)]


def kernel(
    vort, row_hbm, col_mats, twiddle, flips, waves,
    grad, resid,
    rowm, grid_a, grid_u, grid_v, grid_wx, grid_wy, sends, recvs, local_b,
    row_s, col_s, w_spec, previous, adj, next_start, residual,
    dx_t, linv_t, decay_t, nlf_t, flat, grad_v, resid_v,
    table_sem, out_sem, own_sem, send_sem, recv_sem,
):
    me = lax.axis_index("space")
    seg = lax.axis_index("seg")
    after, before = (seg + 1) % 8, (seg + 7) % 8
    rows_in_tile = lax.broadcasted_iota(jnp.int32, (8, LANES), 0)
    first_mask = (rows_in_tile == 0) & (jnp.zeros((8, LANES), jnp.int32) + me == 0)
    others = partners(me)
    both = (0, 1)

    def table_copy(i):
        return pltpu.make_async_copy(row_hbm.at[i], rowm.at[i], table_sem.at[i])

    for i in (0, 3, 2, 1):
        table_copy(i).start()

    barrier = pltpu.get_barrier_semaphore()
    for p in others:
        pl.semaphore_signal(barrier, inc=1, device_id={"space": p}, device_id_type=MESH)
    for s in (after, before):
        for p in others + [me]:
            pl.semaphore_signal(
                barrier, inc=1, device_id={"seg": s, "space": p}, device_id_type=MESH)

    def part(f, g, p):
        return (f, p, pl.ds(GROUP_J[g], 4))

    def own_copy(f, g):
        return pltpu.make_async_copy(
            sends.at[part(f, g, me)], recvs.at[part(f, g, me)], own_sem.at[f, g])

    def start(f, g):
        own_copy(f, g).start()

        def one(p):
            pltpu.make_async_remote_copy(
                src_ref=sends.at[part(f, g, p)], dst_ref=recvs.at[part(f, g, me)],
                send_sem=send_sem.at[f, g], recv_sem=recv_sem.at[f, g],
                device_id={"space": p}, device_id_type=MESH).start()

        if f == 4:
            for p in others:
                pl.when(p < KEPT)(functools.partial(one, p))
        elif f == 5:
            @pl.when(me < KEPT)
            def _():
                for p in others:
                    one(p)
        else:
            for p in others:
                one(p)

    def wait_bytes(f, g, sem, count):
        pltpu.make_async_copy(
            sends.at[part(f, g, pl.ds(0, count))], recvs.at[part(f, g, pl.ds(0, count))],
            sem.at[f, g]).wait()

    def some(f, g, sem):
        @pl.when(me < KEPT)
        def _():
            wait_bytes(f, g, sem, KEPT - 1)

        @pl.when(me >= KEPT)
        def _():
            wait_bytes(f, g, sem, KEPT)

    def inside(f, g, sem):
        @pl.when(me < KEPT)
        def _():
            wait_bytes(f, g, sem, 15)

    def finish(f, g):
        own_copy(f, g).wait()
        kind = {4: inside, 5: some}.get(f)
        if kind:
            kind(f, g, recv_sem)
        else:
            wait_bytes(f, g, recv_sem, 15)

    def finish_send(f, g):
        kind = {4: some, 5: inside}.get(f)
        if kind:
            kind(f, g, send_sem)
        else:
            wait_bytes(f, g, send_sem, 15)

    side = {10: (0, before), 11: (0, after), 12: (4, after)}

    def start_side(f, first=0, last=16):
        source, s = side[f]

        def one(p):
            pltpu.make_async_remote_copy(
                src_ref=sends.at[source, p], dst_ref=recvs.at[f, me],
                send_sem=send_sem.at[f, 0], recv_sem=recv_sem.at[f, 0],
                device_id={"seg": s, "space": p}, device_id_type=MESH).start()

        for p in ([me] + others)[first:last]:
            if f == 12:
                pl.when(p < KEPT)(functools.partial(one, p))
            else:
                one(p)

    def wait_side(f, sem, count=16):
        pltpu.make_async_copy(
            sends.at[side[f][0], pl.ds(0, count)], recvs.at[f, pl.ds(0, count)], sem.at[f, 0]).wait()

    def finish_side(f):
        if f == 12:
            pl.when(me < KEPT)(lambda: wait_side(f, recv_sem))
        else:
            wait_side(f, recv_sem)

    for b in range(16):
        grid_a[b] = vort[:, b * LANES : (b + 1) * LANES].T

    def tiles_of(ref, t):
        return [ref[b, tile(t), :] for b in range(16)]

    def keep(ref, t, tiles):
        for b in range(16):
            ref[b, tile(t), :] = tiles[b]

    loop(16, lambda t: row_short_forward(t, tiles_of(grid_a, t), row_s.at[0]))
    table_copy(0).wait()
    for g in both:
        row_long_forward(g, rowm.at[0], row_s.at[0], sends.at[0])
        if g == 0:
            pl.semaphore_wait(barrier, 47)
        start(0, g)

    def stacked(f):
        return lambda j: sends[f, :, j].reshape(256, LANES)

    def arrived(f):
        return lambda j: recvs[f, :, j].reshape(256, LANES)

    for g in both:
        first = 0 if g == 0 else CHUNK[0]
        ky = waves[0, first : first + CHUNK[g], :] + waves[1, first : first + CHUNK[g], :] * me.astype(F32)

        def make_tables(c, g=g, ky=ky):
            rows = lax.broadcasted_iota(jnp.int32, (CHUNK[g], LANES), 0)
            lanes = lax.broadcasted_iota(jnp.int32, (CHUNK[g], LANES), 1)
            k = 4 * c + 16 * lanes
            for q in range(1, 4):
                k = k + jnp.where(rows >= q * ROWS_OF[g], 1, 0)
            kx = jnp.where(k < N // 2, k, k - N)
            kxf = kx.astype(F32)
            square = kxf * kxf + ky * ky
            decay = jnp.exp(-TIME_STEP * (DRAG + 9.0 * square / (N * N)))
            to = chunk(g, c)
            dx_t[to, :] = jnp.where(kx == -(N // 2), 0.0, kxf)
            linv_t[to, :] = jnp.where(square > 0.0, 1.0 / jnp.maximum(square, 1.0), 0.0)
            decay_t[to, :] = decay
            keep_mask = (3.0 * jnp.abs(kxf) <= N) & (3.0 * jnp.abs(ky) <= N)
            nlf_t[to, :] = jnp.where(keep_mask, TIME_STEP * decay, 0.0)

        loop(4, make_tables, 1)

    def zero_columns(b):
        recvs[5, b] = jnp.zeros((8, 2, 8, LANES), F32)

    @pl.when(me >= KEPT)
    def _():
        def clear(b):
            recvs[4, b] = jnp.zeros((8, 2, 8, LANES), F32)
            recvs[12, b] = jnp.zeros((8, 2, 8, LANES), F32)

        loop(16, clear, 1)

    loop(16 - KEPT, lambda b: zero_columns(b + KEPT), 1)
    flat[...] = jnp.zeros_like(flat)

    def two(re, im):
        return jnp.concatenate([re, im], axis=1)

    def halves(ref, rows):
        return ref[rows, 0:LANES], ref[rows, LANES : 2 * LANES]

    def psi_hat(rows):
        re, im = halves(w_spec, rows)
        linv = linv_t[rows, :]
        return two(linv * re, linv * im)

    def v_hat(rows):
        re, im = halves(w_spec, rows)
        factor = linv_t[rows, :] * dx_t[rows, :]
        return two(factor * im, -factor * re)

    def wx_hat(rows):
        re, im = halves(w_spec, rows)
        factor = dx_t[rows, :]
        return two(-factor * im, factor * re)

    def forward_columns(g, f, emit):
        col_forward(g, recvs.at[f], first_mask, col_mats, twiddle, col_s, emit)

    def inverse_columns(g, f, load):
        col_inverse(g, load, first_mask, col_mats, twiddle, col_s, sends.at[f])
        start(f, g)

    def put(ref):
        def emit(rows, c, value):
            ref[rows, :] = value
        return emit

    for g in both:
        finish(0, g)
        forward_columns(g, 0, put(w_spec))
        inverse_columns(g, 1, psi_hat)
        inverse_columns(g, 2, v_hat)
        inverse_columns(g, 3, wx_hat)

    table_copy(3).wait()
    for g in both:
        row_long_inverse(g, stacked(0), rowm.at[3], row_s.at[0])
    loop(16, lambda t: keep(grid_wy, t, row_short_inverse(t, row_s.at[0])))
    table_copy(2).wait()

    for g in both:
        finish(1, g)
        row_long_inverse(g, arrived(1), rowm.at[3], row_s.at[0])
        if g == 1:
            loop(16, lambda t: keep(grid_u, t, row_short_inverse(t, row_s.at[0])))
        finish(2, g)
        row_long_inverse(g, arrived(2), rowm.at[2], row_s.at[1])
        if g == 1:
            loop(16, lambda t: keep(grid_v, t, row_short_inverse(t, row_s.at[1])))
        if g == 1:
            finish_send(3, 1)
            start_side(10)
            start_side(11, 0, 8)
        finish(3, g)
        row_long_inverse(g, arrived(3), rowm.at[2], row_s.at[2])

    def nonlinear(t):
        tiles = row_short_inverse(t, row_s.at[2])
        product = []
        for b in range(16):
            grid_wx[b, tile(t), :] = tiles[b]
            product.append(
                grid_u[b, tile(t), :] * tiles[b] + grid_v[b, tile(t), :] * grid_wy[b, tile(t), :])
        row_short_forward(t, product, row_s.at[0])

    loop(16, nonlinear)
    for g in both:
        row_long_forward(g, rowm.at[0], row_s.at[0], sends.at[4])
        start(4, g)
    start_side(12)
    table_copy(1).wait()

    finish_side(10)
    for g in both:
        forward_columns(g, 10, put(next_start))

    def own_ky(g):
        rows = slice(0, CHUNK[0]) if g == 0 else slice(CHUNK[0], CHUNK[0] + CHUNK[1])
        return waves[0, rows, :] + waves[1, rows, :] * me.astype(F32)

    def end_of(g, rows, ref, value):
        re, im = halves(ref, rows)
        decay, nlf = decay_t[rows, :], nlf_t[rows, :]
        forced = (dx_t[rows, :] == 0.0) & (nlf > 0.0) & (own_ky(g) == float(FORCING_WAVE))
        force = jnp.where(forced, TIME_STEP * FORCE_AMP * (N * N / 2.0) * decay, 0.0)
        return (
            decay * re - nlf * value[:, 0:LANES] + force,
            decay * im - nlf * value[:, LANES : 2 * LANES],
        )

    def put_adjoint(g):
        def emit(rows, c, value):
            end_re, end_im = end_of(g, rows, w_spec, value)
            next_re, next_im = halves(next_start, rows)
            adj[rows, :] = two(end_re - next_re, end_im - next_im)
        return emit

    def weight_hat(rows):
        re, im = halves(adj, rows)
        nlf = nlf_t[rows, :]
        return two(nlf * re, nlf * im)

    for g in both:
        finish(4, g)
        forward_columns(g, 4, put_adjoint(g))
        inverse_columns(g, 5, weight_hat)
    start_side(11, 8, 16)

    for g in both:
        finish(5, g)
        row_long_inverse(g, arrived(5), rowm.at[2], row_s.at[0])

    def weighted(t):
        tiles = row_short_inverse(t, row_s.at[0])
        keep(grid_a, t, tiles)
        row_short_forward(t, [tiles[b] * grid_u[b, tile(t), :] for b in range(16)], row_s.at[1])

    def product(ref, scratch):
        def step(t):
            tiles = [grid_a[b, tile(t), :] * ref[b, tile(t), :] for b in range(16)]
            row_short_forward(t, tiles, scratch)
        return step

    loop(16, weighted)
    for g in both:
        row_long_forward(g, rowm.at[0], row_s.at[1], sends.at[6])
        start(6, g)
    for f, ref, mat in ((7, grid_wx, 1), (8, grid_wy, 0)):
        loop(16, product(ref, row_s.at[0]))
        for g in both:
            row_long_forward(g, rowm.at[mat], row_s.at[0], sends.at[f])
            start(f, g)
    loop(16, product(grid_v, row_s.at[0]))
    for g in both:
        row_long_forward(g, rowm.at[1], row_s.at[0], local_b)

    def put_residual(g):
        def emit(rows, c, value):
            prev_re, prev_im = end_of(g, rows, previous, value)
            re, im = halves(w_spec, rows)
            res_re, res_im = prev_re - re, prev_im - im
            residual[rows, :] = two(res_re, res_im)
            adj_re, adj_im = halves(adj, rows)
            decay = decay_t[rows, :]
            adj[rows, :] = two(decay * adj_re - res_re, decay * adj_im - res_im)
        return emit

    finish_side(11)
    for g in both:
        forward_columns(g, 11, put(previous))
    finish_side(12)
    for g in both:
        forward_columns(g, 12, put_residual(g))

    slots = slot_table()

    def write_residual(k, mirror, flip):
        for part in range(2):
            lanes = slice(part * LANES, (part + 1) * LANES)
            for j in range(8):
                direct = residual[tile_rows(k, j), lanes]
                mirrored = residual[tile_rows(mirror, j), lanes]
                if part:
                    mirrored = -mirrored
                for h in range(2):
                    to = int(slots[j, 4 * h])
                    flat[part, 0, pl.ds(to, 4, stride=16), :] = direct[4 * h : 4 * h + 4]
                    flat[part, 1, pl.ds(64 + to, 4, stride=16), :] = mirrored[4 * h : 4 * h + 4]
            extra = residual[tile_rows(k, 8), lanes]
            flat[part, 0, 64:72, :] = jnp.where(first_mask, extra, 0.0)
            flat[part, 1, 64:72, :] = jnp.where(first_mask, 0.0, flat[part, 1, 64:72, :])
            high, low = split(jnp.concatenate([flat[part, 0], flat[part, 1]], axis=1))
            contract = (((1,), (1,)), ((), ()))
            result = lax.dot_general(flip, high, contract, preferred_element_type=F32)
            result = result + lax.dot_general(flip, low, contract, preferred_element_type=F32)
            resid_v[part, :, k, :] = result

    write_residual(0, 0, flips[0])
    loop(15, lambda i: write_residual(i + 1, 15 - i, flips[1]), 1)
    resid_copy = pltpu.make_async_copy(resid_v, resid, out_sem.at[0])
    resid_copy.start()

    def add_a(rows, c, value):
        re, im = halves(adj, rows)
        dx = dx_t[rows, :]
        adj[rows, :] = two(re - dx * value[:, LANES : 2 * LANES], im + dx * value[:, 0:LANES])

    def add_c(rows, c, value):
        re, im = halves(adj, rows)
        linv = linv_t[rows, :]
        adj[rows, :] = two(re + linv * value[:, 0:LANES], im + linv * value[:, LANES : 2 * LANES])

    def add_d(rows, c, value):
        re, im = halves(adj, rows)
        factor = linv_t[rows, :] * dx_t[rows, :]
        adj[rows, :] = two(
            re + factor * value[:, LANES : 2 * LANES], im - factor * value[:, 0:LANES])

    for f, emit in ((6, add_a), (7, add_c), (8, add_d)):
        for g in both:
            finish(f, g)
            forward_columns(g, f, emit)
            if f == 8:
                inverse_columns(g, 9, lambda rows: adj[rows, :])

    def total(j):
        return (recvs[9, :, j] + local_b[:, j]).reshape(256, LANES)

    for g in both:
        finish(9, g)
        row_long_inverse(g, total, rowm.at[2], row_s.at[0])
    loop(16, lambda t: keep(grid_a, t, row_short_inverse(t, row_s.at[0])))
    for b in range(16):
        grad_v[:, b * LANES : (b + 1) * LANES] = grid_a[b].T
    grad_copy = pltpu.make_async_copy(grad_v, grad, out_sem.at[1])
    grad_copy.start()
    for f in range(10):
        for g in both:
            if (f, g) != (3, 1):
                finish_send(f, g)
    wait_side(10, send_sem)
    wait_side(11, send_sem)
    wait_side(12, send_sem, KEPT)
    resid_copy.wait()
    grad_copy.wait()


def body(vorticity):
    col_mats, twiddle = col_tables()
    vmem = pl.BlockSpec(memory_space=pltpu.VMEM)
    hbm = pl.BlockSpec(memory_space=pl.ANY)
    slab = (16, 8, 2, 8, LANES)
    grid = pltpu.VMEM((16, LANES, LANES), F32)
    spectrum = pltpu.VMEM((ALL_ROWS, 2 * LANES), F32)
    factor = pltpu.VMEM((ALL_ROWS, LANES), F32)
    outs = ((LANES, N), (2, LANES, 16, LANES))
    gradient, residual = pl.pallas_call(
        kernel,
        out_shape=tuple(jax.ShapeDtypeStruct(shape, F32) for shape in outs),
        in_specs=[vmem, hbm, vmem, vmem, vmem, vmem],
        out_specs=(hbm, hbm),
        scratch_shapes=[
            pltpu.VMEM((4, 2, 8, 256, 256), BF16),
            grid, grid, grid, grid, grid,
            pltpu.VMEM((10,) + slab, F32),
            pltpu.VMEM((13,) + slab, F32),
            pltpu.VMEM(slab, F32),
            pltpu.VMEM((3, 8, 256, LANES), F32),
            spectrum, spectrum, spectrum, spectrum, spectrum, spectrum,
            factor, factor, factor, factor,
            pltpu.VMEM((2, 2, LANES, LANES), F32),
            pltpu.VMEM(outs[0], F32),
            pltpu.VMEM(outs[1], F32),
            pltpu.SemaphoreType.DMA((4,)),
            pltpu.SemaphoreType.DMA((2,)),
            pltpu.SemaphoreType.DMA((10, 2)),
            pltpu.SemaphoreType.DMA((13, 2)),
            pltpu.SemaphoreType.DMA((13, 2)),
        ],
        compiler_params=pltpu.CompilerParams(
            collective_id=0, has_side_effects=True, vmem_limit_bytes=62 * 2**20
        ),
        name="orbit_gradient",
    )(vorticity[0], jnp.asarray(row_tables()), jnp.asarray(col_mats), jnp.asarray(twiddle),
      jnp.asarray(flip_tables()), jnp.asarray(wave_table()))
    return gradient[None], residual.reshape(1, 2, N, LANES)


def solution(mesh):
    return jax.shard_map(
        body,
        mesh=mesh,
        in_specs=(P("seg", "space", None),),
        out_specs=(P("seg", "space", None), P("seg", None, None, "space")),
        check_vma=False,
    )
```
